256 devices in a mesh: span: 16 (over z, core), qry: 16 (over y, x).
Axes of the slice: x: 4, y: 4, z: 8, core: 2. Of those that a mesh axis runs over, the one named last changes fastest.
Arguments:
- features: bfloat16 [16, 32, 128, 256], P('span', 'qry'), may hold values from -6 to 6
- conv_weight: bfloat16 [27, 256, 256], replicated, may hold values from -0.078125 to 0.078125
- queries: float32 [128, 256], P('qry'), may hold values from -600 to 600
- w_query: bfloat16 [2, 256, 256], replicated, may hold values from -0.26171875 to 0.26171875
- w_key: bfloat16 [2, 256, 256], replicated, may hold values from -0.26171875 to 0.26171875
- w_value: bfloat16 [2, 256, 256], replicated, may hold values from -0.26171875 to 0.26171875
- w_out: bfloat16 [2, 256, 256], replicated, may hold values from -0.26171875 to 0.26171875
- norm_gain: float32 [256], replicated, may hold values from 0.5 to 1.5
- mask_weight: bfloat16 [256, 256], replicated, may hold values from -0.375 to 0.375
- mask_blocks: int32 [128, 4], replicated, may hold values from 0 to 511, as said below
Outputs:
- query_embed: float32 [128, 256], P('qry')
- mask_logits: bfloat16 [128, 16, 32, 128], P(None, 'span', 'qry')
The draws below stay inside these ranges and needn't reach their ends.
Inputs may be any that keep to these rules, and one draw needn't show every extreme that they name: `mask_blocks`: each row lists 4 distinct mask blocks, block z * 32 + y being the voxels pixel[z, y, :]; no block appears twice in the whole array.
All inputs are finite; a program needn't handle non-finite values.
Results may differ from the reference program's by a relative error of at most 0.04.
The reference program's roundings to bfloat16 on the way (of `pixel`, `qproj`, `attn` and `mask_embed`) count: a program that leaves them out, or rounds other values in their place, can miss the bound.
Values may be sent and summed in bfloat16 or wider, within the bound.
A program may use at most 64 MiB of HBM per device.

```python
import jax
import jax.numpy as jnp
from jax import lax

D = 256
HEADS = 8
HEAD_DIM = 32
LAYERS = 2
MB = 4
NX = 128
NZ = 16
NY = 32
NBLK = 512
NQ = 128


def draw_queries(key, part):
    first_key = jax.random.fold_in(key, 0)
    values = jnp.clip(jax.random.normal(first_key, (NQ, D), jnp.float32), -6.0, 6.0)
    return values.astype(jnp.float32)


def draw_mask_blocks(key, part):
    order = jax.random.permutation(jax.random.fold_in(key, 17), NBLK)
    return order[:NQ * MB].reshape(NQ, MB).astype(jnp.int32)


def block_levels(rng, dims, shards, smallest, largest):
    gain, own = 1.0, jax.random.fold_in(rng, 6)
    for dim, blocks in shards:
        heights = jnp.exp(jax.random.uniform(jax.random.fold_in(own, dim), (blocks,), jnp.float32, smallest / len(shards), largest / len(shards)))
        gain = gain * jnp.repeat(heights, dims[dim] // blocks).reshape([-1 if axis == dim else 1 for axis in range(len(dims))])
    return gain


def bell_draw(stream_key, shape, width, reach, pieces=(), held_as=jnp.bfloat16):
    gain = block_levels(stream_key, shape, pieces, -0.22, 0.18) if pieces else 1.0
    drawn = jax.random.normal(stream_key, shape, jnp.float32) * width * gain
    return jnp.minimum(jnp.maximum(drawn, -reach), reach).astype(held_as)


def setup_inputs(seed: int = 0) -> dict:
    seeds = jax.random.split(jax.random.key(seed), 11)
    return {
        "features": bell_draw(seeds[0], (NZ, NY, NX, D), 1.0, 6.0, ((0, 16), (1, 16))),
        "conv_weight": bell_draw(seeds[1], (27, D, D), (27 * D) ** -0.5, 0.078125),
        "queries": draw_queries(jax.random.fold_in(seeds[10], 71), 0),
        "w_query": jnp.clip(jax.random.uniform(seeds[3], (LAYERS, D, D), jnp.float32, -0.26171875, 0.26171875), -0.26171875, 0.26171875).astype(jnp.bfloat16),
        "w_key": jnp.clip(jax.random.uniform(seeds[4], (LAYERS, D, D), jnp.float32, -0.26171875, 0.26171875), -0.26171875, 0.26171875).astype(jnp.bfloat16),
        "w_value": jnp.clip(jax.random.uniform(seeds[5], (LAYERS, D, D), jnp.float32, -0.26171875, 0.26171875), -0.26171875, 0.26171875).astype(jnp.bfloat16),
        "w_out": jnp.clip(jax.random.uniform(seeds[6], (LAYERS, D, D), jnp.float32, -0.26171875, 0.26171875), -0.26171875, 0.26171875).astype(jnp.bfloat16),
        "norm_gain": jnp.clip(1.0 + 0.1 * jax.random.normal(seeds[7], (D,), jnp.float32), 0.5, 1.5),
        "mask_weight": bell_draw(seeds[8], (D, D), D ** -0.5, 0.375),
        "mask_blocks": draw_mask_blocks(jax.random.fold_in(seeds[10], 71), 0),
    }


def reference(features, conv_weight, queries, w_query, w_key, w_value, w_out, norm_gain, mask_weight, mask_blocks):
    padded = jnp.pad(features, ((1, 1), (1, 1), (1, 1), (0, 0)))

    def plane(z_index):
        slab = lax.dynamic_slice_in_dim(padded, z_index, 3, 0)
        total = jnp.zeros((NY * NX, D), jnp.float32)
        for depth_off in range(3):
            for row_off in range(3):
                for col_off in range(3):
                    tap = slab[depth_off, row_off:row_off + NY, col_off:col_off + NX].reshape(NY * NX, D)
                    total = total + jnp.dot(tap, conv_weight[9 * depth_off + 3 * row_off + col_off], preferred_element_type=jnp.float32)
        return jnp.maximum(total, 0.0).astype(jnp.bfloat16).reshape(NY, NX, D)
    pixel = lax.map(plane, jnp.arange(NZ, dtype=jnp.int32))
    flat = pixel.reshape(NZ * NY * NX, D)
    state = queries
    scale = HEAD_DIM ** (-0.5)
    for layer_index in range(LAYERS):
        qproj = (jnp.dot(state.astype(jnp.bfloat16), w_query[layer_index], preferred_element_type=jnp.float32) * scale).astype(jnp.bfloat16)
        keys = jnp.dot(flat, w_key[layer_index], preferred_element_type=jnp.float32).astype(jnp.bfloat16).reshape(NBLK, NX, D)
        values = jnp.dot(flat, w_value[layer_index], preferred_element_type=jnp.float32).astype(jnp.bfloat16).reshape(NBLK, NX, D)
        picked_keys = keys[mask_blocks].reshape(NQ, MB * NX, HEADS, HEAD_DIM).astype(jnp.float32)
        picked_values = values[mask_blocks].reshape(NQ, MB * NX, HEADS, HEAD_DIM).astype(jnp.float32)
        scores = jnp.einsum('nhe,nvhe->nhv', qproj.reshape(NQ, HEADS, HEAD_DIM).astype(jnp.float32), picked_keys)
        top = lax.optimization_barrier(jnp.max(scores, axis=-1, keepdims=True))
        prob = jnp.exp(scores - top)
        total = lax.optimization_barrier(jnp.sum(prob, axis=-1))
        weighted = jnp.einsum('nhv,nvhe->nhe', prob.astype(jnp.bfloat16).astype(jnp.float32), picked_values)
        attn = (weighted / total[:, :, None]).reshape(NQ, D).astype(jnp.bfloat16)
        state = state + jnp.dot(attn, w_out[layer_index], preferred_element_type=jnp.float32)
    mean = lax.optimization_barrier(jnp.mean(state, axis=-1, keepdims=True))
    centered = state - mean
    var = lax.optimization_barrier(jnp.mean(centered * centered, axis=-1, keepdims=True))
    query_embed = centered * lax.rsqrt(var + 1e-05) * norm_gain
    mask_embed = jnp.dot(query_embed.astype(jnp.bfloat16), mask_weight, preferred_element_type=jnp.float32).astype(jnp.bfloat16)
    logits = jnp.einsum('nd,vd->nv', mask_embed, flat, preferred_element_type=jnp.float32) * D ** (-0.5)
    mask_logits = logits.astype(jnp.bfloat16).reshape(NQ, NZ, NY, NX)
    return (query_embed, mask_logits)
```

```python
import jax
import jax.numpy as jnp
from jax import lax
from jax.experimental import pallas as pl
from jax.experimental.pallas import tpu as pltpu
from jax.sharding import PartitionSpec as P

MESH = pl.DeviceIdType.MESH
HEADS = 8
LAYERS = 2
D = 256
HEAD_DIM = 32
NX = 128
NQ = 128
MB = 4
NY = 32
SPAN = 16
QRY = 16
F32 = jnp.float32
BF16 = jnp.bfloat16
MSG = 80


def iota(shape, dim):
    return lax.broadcasted_iota(jnp.int32, shape, dim)


def dot(a, b):
    return jnp.dot(a, b, preferred_element_type=F32)


def dot_nt(a, b):
    return lax.dot_general(a, b, (((1,), (1,)), ((), ())), preferred_element_type=F32)


def wrap(i, n):
    return lax.rem(i + n, n)


def merge(ids, block):
    rows = ids.shape[0]
    outs = jnp.concatenate(
        [block[:, half * 32 : half * 32 + 32, :].reshape(QRY * 32, 128) for half in range(2)], axis=1
    )
    terms = block[:, 64:MSG, :].reshape(QRY * 16, 128)
    col = iota((rows, QRY * 32), 1)
    pair_id = (col % 16) * NY + (col // 32) * 2 + (col // 16) % 2
    row = iota((rows, QRY * 16), 1)
    kind = row % 16
    term_y = jnp.where(kind < 6, (row // 16) * 2 + jnp.where(kind < 3, 0, 1), -1)
    lane_z = iota((rows, 128), 1) // HEADS
    pick, term = [], []
    for j in range(MB):
        idj = ids[:, j : j + 1]
        pick.append(jnp.where(pair_id == idj, 1.0, 0.0).astype(BF16))
        term.append(jnp.where(term_y == idj % NY, 1.0, 0.0).astype(BF16))
    chosen = dot(jnp.concatenate(pick, axis=0), outs)
    lse = dot(jnp.concatenate(term, axis=0), terms)
    lses = []
    for j in range(MB):
        lj = jnp.where(lane_z == ids[:, j : j + 1] // NY, lse[j * rows : (j + 1) * rows], 0.0)
        for shift in (8, 16, 32, 64):
            lj = lj + pltpu.roll(lj, shift, axis=1)
        lses.append(lj)
    top = jnp.maximum(jnp.maximum(lses[0], lses[1]), jnp.maximum(lses[2], lses[3]))
    weights = [jnp.exp(lj - top) for lj in lses]
    inv = 1.0 / (weights[0] + weights[1] + weights[2] + weights[3])
    attn = jnp.zeros((rows, D), F32)
    for j in range(MB):
        wj = weights[j] * inv
        attn = attn + jnp.concatenate([wj, wj], axis=1) * chosen[j * rows : (j + 1) * rows]
    return attn


def kernel(
    feat_hbm, conv_hbm, queries_hbm, wq_hbm, wk_hbm, wv_hbm, wo_hbm, gain_ref, mw_hbm, mb_ref,
    embed_ref, logit_ref,
    ext, taps, qbuf, wq, wk, wv, wo, mw, wvp, wop, pix, keys, vals, stage1, stage2, state,
    local_sem, conv_sem, halo_send, halo_recv, q_send, q_recv, s_send, s_recv, y_send, y_recv,
):
    s = lax.axis_index("span")
    q = lax.axis_index("qry")
    up, down = wrap(s + 1, SPAN), wrap(s - 1, SPAN)
    right, left = wrap(q + 1, QRY), wrap(q - 1, QRY)

    own = pltpu.make_async_copy(feat_hbm.at[0], ext.at[1, pl.ds(1, 2)], local_sem.at[0])
    own.start()
    own_q = pltpu.make_async_copy(queries_hbm, qbuf.at[q], local_sem.at[1])
    own_q.start()
    loads = []
    for k, (src, dst) in enumerate(
        ((wv_hbm, wv), (wo_hbm, wo), (wq_hbm, wq), (wk_hbm, wk), (mw_hbm, mw))
    ):
        loads.append(pltpu.make_async_copy(src, dst, local_sem.at[2 + k]))
        loads[-1].start()
    conv_loads = [
        pltpu.make_async_copy(conv_hbm.at[:, dx], taps.at[dx], conv_sem.at[dx]) for dx in range(3)
    ]
    for load in conv_loads:
        load.start()

    barrier = pltpu.get_barrier_semaphore()
    corners = ((up, right), (up, left), (down, right), (down, left))
    for peer in corners:
        pl.semaphore_signal(barrier, inc=1, device_id=peer, device_id_type=MESH)
    for d in range(1, SPAN):
        pl.semaphore_signal(barrier, inc=1, device_id=(wrap(s + d, SPAN), q), device_id_type=MESH)
    for d in range(1, QRY):
        pl.semaphore_signal(barrier, inc=1, device_id=(s, wrap(q + d, QRY)), device_id_type=MESH)
    pl.semaphore_wait(barrier, len(corners) + SPAN - 1 + QRY - 1)

    own.wait()
    sends = []
    both, first, last = ext.at[1, pl.ds(1, 2)], ext.at[1, 1], ext.at[1, 2]
    for k, (src, dst, peer) in enumerate(
        (
            (last, ext.at[0, 0], (up, right)),
            (first, ext.at[0, 3], (up, left)),
            (last, ext.at[2, 0], (down, right)),
            (first, ext.at[2, 3], (down, left)),
            (both, ext.at[0, pl.ds(1, 2)], (up, q)),
            (both, ext.at[2, pl.ds(1, 2)], (down, q)),
            (last, ext.at[1, 0], (s, right)),
            (first, ext.at[1, 3], (s, left)),
        )
    ):
        copy = pltpu.make_async_remote_copy(
            src_ref=src, dst_ref=dst, send_sem=halo_send.at[k], recv_sem=halo_recv.at[k],
            device_id=peer, device_id_type=MESH,
        )
        copy.start()
        sends.append(copy)

    def to_all(buf, me, send_sem, recv_sem, along_span):
        n = SPAN if along_span else QRY
        for d in range(1, n):
            peer = (wrap(s + d, n), q) if along_span else (s, wrap(q + d, n))
            pltpu.make_async_remote_copy(
                src_ref=buf.at[me], dst_ref=buf.at[me], send_sem=send_sem, recv_sem=recv_sem,
                device_id=peer, device_id_type=MESH,
            ).start()

    def wait_all(buf, sem):
        most = buf.at[pl.ds(0, buf.shape[0] - 1)]
        pltpu.make_async_copy(most, most, sem).wait()

    own_q.wait()
    to_all(qbuf, q, q_send, q_recv, False)

    perm = jnp.where(
        iota((D, D), 1) == (iota((D, D), 0) % HEAD_DIM) * HEADS + iota((D, D), 0) // HEAD_DIM, 1.0, 0.0
    ).astype(BF16)
    perm_t = jnp.where(
        iota((D, D), 0) == (iota((D, D), 1) % HEAD_DIM) * HEADS + iota((D, D), 1) // HEAD_DIM, 1.0, 0.0
    ).astype(BF16)
    for load in loads:
        load.wait()
    for layer in range(LAYERS):
        wvp[layer] = dot(wv[layer], perm).astype(BF16)
        wop[layer] = dot(perm_t, wo[layer]).astype(BF16)
    for load in conv_loads:
        load.wait()

    for copy in sends:
        copy.wait_recv()

    @pl.when(s == 0)
    def _():
        ext[0] = jnp.zeros((4, NX, D), BF16)

    @pl.when(s == SPAN - 1)
    def _():
        ext[2] = jnp.zeros((4, NX, D), BF16)

    @pl.when(q == 0)
    def _():
        ext[:, 0] = jnp.zeros((3, NX, D), BF16)

    @pl.when(q == QRY - 1)
    def _():
        ext[:, 3] = jnp.zeros((3, NX, D), BF16)

    slab = jnp.concatenate(
        [ext[dz, dy : dy + 2].reshape(2 * NX, D) for dz in range(3) for dy in range(3)], axis=1
    )
    x_at = iota((2 * NX, D), 0) % NX
    before = dot(slab, taps[0].reshape(9 * D, D))
    conv = jnp.where(x_at == 0, 0.0, pltpu.roll(before, 1, axis=0))
    conv = conv + dot(slab, taps[1].reshape(9 * D, D))
    after = dot(slab, taps[2].reshape(9 * D, D))
    conv = conv + jnp.where(x_at == NX - 1, 0.0, pltpu.roll(after, 2 * NX - 1, axis=0))
    pixel = jnp.maximum(conv, 0.0).astype(BF16)
    pix[...] = pixel
    for layer in range(LAYERS):
        keys[layer] = dot(pixel, wk[layer]).astype(BF16)
        vals[layer] = dot(pixel, wvp[layer]).astype(BF16)

    wait_all(qbuf, q_recv)
    all_ids = mb_ref[...]
    state_all = qbuf[...].reshape(NQ, D)
    own_ids, own_state = [], []
    for r in range(2):
        block_id = s * NY + q * 2 + r
        lists = jnp.max(jnp.where(all_ids == block_id, 1, 0), axis=1, keepdims=True) > 0
        own_ids.append(jnp.sum(jnp.where(lists, all_ids.astype(F32), 0.0), axis=0, keepdims=True))
        own_state.append(jnp.sum(jnp.where(lists, state_all, 0.0), axis=0, keepdims=True))
    own_ids = jnp.concatenate(own_ids + [jnp.full((6, MB), -1.0, F32)], axis=0).astype(jnp.int32)
    own_state = jnp.concatenate(own_state + [jnp.zeros((6, D), F32)], axis=0)

    head_of = iota((HEADS, D), 1) // HEAD_DIM == iota((HEADS, D), 0)
    head_of_lane = iota((HEADS, D), 1) % HEADS == iota((HEADS, D), 0)
    lse_lane = iota((HEADS, 128), 1) == s * HEADS + iota((HEADS, 128), 0)
    for layer in range(LAYERS):
        qproj = (dot(own_state.astype(BF16), wq[layer]) * HEAD_DIM**-0.5).astype(BF16).astype(F32)
        spread = jnp.concatenate(
            [jnp.where(head_of, qproj[r : r + 1], 0.0) for r in range(2)], axis=0
        ).astype(BF16)
        scores = dot_nt(spread, keys[layer])
        scores = jnp.concatenate([scores[0:8, 0:NX], scores[8:16, NX : 2 * NX]], axis=0)
        top = jnp.max(scores, axis=1, keepdims=True)
        prob = jnp.exp(scores - top)
        total = jnp.sum(prob, axis=1, keepdims=True)
        inv = 1.0 / total
        lse = top + jnp.log(total)
        prob = prob.astype(BF16)
        low, high, lines = [], [], []
        for r in range(2):
            part = slice(r * HEADS, (r + 1) * HEADS)
            weighted = dot(prob[part], vals[layer, r * NX : (r + 1) * NX])
            out = jnp.sum(jnp.where(head_of_lane, weighted * inv[part], 0.0), axis=0, keepdims=True)
            low.append(out[:, 0:128])
            high.append(out[:, 128:256])
            lines.append(jnp.sum(jnp.where(lse_lane, lse[part], 0.0), axis=0, keepdims=True))
        buf1, buf2 = stage1.at[layer], stage2.at[layer]
        buf1[s] = jnp.concatenate(low + high + lines + [jnp.zeros((2, 128), F32)], axis=0)
        to_all(buf1, s, s_send.at[layer], s_recv.at[layer], True)
        if layer == 1:
            attn = merge(all_ids, stage2[0])
            state[...] = state_all + dot(attn.astype(BF16), wop[0])
        wait_all(buf1, s_recv.at[layer])
        got = stage1[layer]
        message = [got[:, k, :] for k in range(4)]
        for r in range(2):
            line = jnp.sum(got[:, 4 + r, :], axis=0, keepdims=True)
            for _ in range(3):
                term = line.astype(BF16).astype(F32)
                message.append(term)
                line = line - term
        message.append(jnp.zeros((10, 128), F32))
        buf2[q] = jnp.concatenate(message, axis=0).astype(BF16)
        to_all(buf2, q, y_send.at[layer], y_recv.at[layer], False)
        wait_all(buf2, y_recv.at[layer])
        if layer == 0:
            attn = merge(own_ids, stage2[0])
            own_state = own_state + dot(attn.astype(BF16), wop[0])

    attn = merge(all_ids, stage2[1])
    final = state[...] + dot(attn.astype(BF16), wop[1])
    mean = jnp.mean(final, axis=-1, keepdims=True)
    centered = final - mean
    var = jnp.mean(centered * centered, axis=-1, keepdims=True)
    embed = centered * lax.rsqrt(var + 1e-05) * gain_ref[...]
    state[...] = embed
    embed_ref[...] = state[pl.ds(pl.multiple_of(q * 8, 8), 8), :]
    mask_embed = dot(embed.astype(BF16), mw[...]).astype(BF16)
    logit_ref[...] = (dot_nt(mask_embed, pix[...]) * D**-0.5).astype(BF16)

    for copy in sends:
        copy.wait_send()
    wait_all(qbuf, q_send)
    for layer in range(LAYERS):
        wait_all(stage1.at[layer], s_send.at[layer])
        wait_all(stage2.at[layer], y_send.at[layer])


def local(
    features, conv_weight, queries, w_query, w_key, w_value, w_out, norm_gain, mask_weight, mask_blocks
):
    anywhere = pl.BlockSpec(memory_space=pl.ANY)
    vmem = pl.BlockSpec(memory_space=pltpu.VMEM)
    dma = pltpu.SemaphoreType.DMA
    square = pltpu.VMEM((LAYERS, D, D), BF16)
    embed, logits = pl.pallas_call(
        kernel,
        out_shape=(
            jax.ShapeDtypeStruct((8, D), F32),
            jax.ShapeDtypeStruct((NQ, 2 * NX), BF16),
        ),
        in_specs=[anywhere] * 7 + [vmem, anywhere, vmem],
        out_specs=(vmem, vmem),
        scratch_shapes=[
            pltpu.VMEM((3, 4, NX, D), BF16),
            pltpu.VMEM((3, 9, D, D), BF16),
            pltpu.VMEM((QRY, 8, D), F32),
            square,
            square,
            square,
            square,
            pltpu.VMEM((D, D), BF16),
            square,
            square,
            pltpu.VMEM((2 * NX, D), BF16),
            square,
            square,
            pltpu.VMEM((LAYERS, SPAN, 8, 128), F32),
            pltpu.VMEM((LAYERS, QRY, MSG, 128), BF16),
            pltpu.VMEM((NQ, D), F32),
            dma((7,)),
            dma((3,)),
            dma((8,)),
            dma((8,)),
            dma,
            dma,
            dma((LAYERS,)),
            dma((LAYERS,)),
            dma((LAYERS,)),
            dma((LAYERS,)),
        ],
        compiler_params=pltpu.CompilerParams(
            collective_id=0, has_side_effects=True, vmem_limit_bytes=40 * 1024 * 1024
        ),
    )(
        features,
        conv_weight.reshape(9, 3, D, D),
        queries,
        w_query,
        w_key,
        w_value,
        w_out,
        norm_gain.reshape(1, D),
        mask_weight,
        mask_blocks,
    )
    return embed, logits.reshape(NQ, 1, 2, NX)


def solution(mesh):
    return jax.shard_map(
        local,
        mesh=mesh,
        in_specs=(
            P("span", "qry", None, None),
            P(),
            P("qry", None),
            P(),
            P(),
            P(),
            P(),
            P(),
            P(),
            P(),
        ),
        out_specs=(P("qry", None), P(None, "span", "qry", None)),
        check_vma=False,
    )
```

```python
import jax
import jax.numpy as jnp
from jax import lax
from jax.experimental import pallas as pl
from jax.experimental.pallas import tpu as pltpu
from jax.sharding import PartitionSpec as P

MESH = pl.DeviceIdType.MESH
HEADS = 8
LAYERS = 2
D = 256
HEAD_DIM = 32
NX = 128
NQ = 128
MB = 4
NY = 32
SPAN = 16
QRY = 16
F32 = jnp.float32
BF16 = jnp.bfloat16
ZS = 8
NEAR_ROWS = 32
FAR_ROWS = 48
Z_ORDER = (0, 1, 7, 2, 6, 3, 5, 4)
Z_SENDS = (4, 3, 5, 2, 6, 1, 7)
XY_SENDS = sorted(
    ((dy, dx) for dy in range(4) for dx in range(4) if dy or dx),
    key=lambda t: -(min(t[0], 4 - t[0]) + min(t[1], 4 - t[1])),
)


def iota(shape, dim):
    return lax.broadcasted_iota(jnp.int32, shape, dim)


def dot(a, b):
    return jnp.dot(a, b, preferred_element_type=F32)


def dot_nt(a, b):
    return lax.dot_general(a, b, (((1,), (1,)), ((), ())), preferred_element_type=F32)


def wrap(i, n):
    return lax.rem(i + n, n)


def slot_plane(slot, z):
    place = slot // 2
    offset = jnp.zeros_like(slot)
    for k, dz in enumerate(Z_ORDER):
        offset = jnp.where(place == k, dz, offset)
    return ((z + offset) % ZS) * 2 + slot % 2


def merge(ids, near, far, pair_id, term_y, lane_z):
    rows = ids.shape[0]
    outs = jnp.concatenate(
        [
            jnp.concatenate(
                [part[:, half * 16 : half * 16 + 16, :].reshape(QRY * 16, 128) for half in range(2)],
                axis=1,
            )
            for part in (near, far)
        ],
        axis=0,
    )
    terms = far[:, 32:FAR_ROWS, :].reshape(QRY * 16, 128)
    pick, term = [], []
    for j in range(MB):
        idj = ids[:, j : j + 1]
        pick.append(jnp.where(pair_id == idj, 1.0, 0.0).astype(BF16))
        term.append(jnp.where(term_y == idj % NY, 1.0, 0.0).astype(BF16))
    lse = dot(jnp.concatenate(term, axis=0), terms)
    chosen = dot(jnp.concatenate(pick, axis=0), outs)
    lses = []
    for j in range(MB):
        lj = jnp.where(lane_z == ids[:, j : j + 1] // NY, lse[j * rows : (j + 1) * rows], 0.0)
        for shift in (8, 16, 32, 64):
            lj = lj + pltpu.roll(lj, shift, axis=1)
        lses.append(lj)
    top = jnp.maximum(jnp.maximum(lses[0], lses[1]), jnp.maximum(lses[2], lses[3]))
    weights = [jnp.exp(lj - top) for lj in lses]
    inv = 1.0 / (weights[0] + weights[1] + weights[2] + weights[3])
    attn = jnp.zeros((rows, D), F32)
    for j in range(MB):
        wj = weights[j] * inv
        attn = attn + jnp.concatenate([wj, wj], axis=1) * chosen[j * rows : (j + 1) * rows]
    return attn


def kernel(
    feat_hbm, conv_hbm, queries_hbm, wq_hbm, wk_hbm, wv_hbm, wo_hbm, gain_hbm, mw_hbm, mb_hbm,
    embed_ref, logit_ref,
    ext, taps, qbuf, qpbuf, wq, wk, wv, wo, mw, gain, mb, wvp, wop, pix, keys, vals,
    stage1, near, far, state,
    local_sem, conv_sem, halo_send, halo_recv, q_send, q_recv, p_send, p_recv,
    s_send, s_recv, y_send, y_recv,
):
    s = lax.axis_index("span")
    q = lax.axis_index("qry")
    z, core = s // 2, lax.rem(s, 2)
    y, x = q // 4, lax.rem(q, 4)
    up, down = wrap(s + 1, SPAN), wrap(s - 1, SPAN)
    right, left = wrap(q + 1, QRY), wrap(q - 1, QRY)
    z_peers = [(d, c) for d in Z_SENDS for c in range(2)] + [(0, 1)]
    z_index = [wrap(z + d, ZS) * 2 + (c if d else 1 - core) for d, c in z_peers]
    xy_index = [lax.rem(y + dy, 4) * 4 + lax.rem(x + dx, 4) for dy, dx in XY_SENDS]

    barrier = pltpu.get_barrier_semaphore()
    for plane in z_index[::-1]:
        pl.semaphore_signal(barrier, inc=1, device_id=(plane, q), device_id_type=MESH)
    for block in xy_index[::-1]:
        pl.semaphore_signal(barrier, inc=1, device_id=(s, block), device_id_type=MESH)

    own = pltpu.make_async_copy(feat_hbm.at[0], ext.at[1, pl.ds(1, 2)], local_sem.at[0])
    own.start()
    early, loads = [], []
    for k, (src, dst) in enumerate(
        (
            (mb_hbm, mb),
            (queries_hbm, qbuf.at[q]),
            (wq_hbm, wq),
            (wv_hbm, wv),
            (wo_hbm, wo),
            (wk_hbm, wk),
            (mw_hbm, mw),
            (gain_hbm, gain),
        )
    ):
        copy = pltpu.make_async_copy(src, dst, local_sem.at[1 + k])
        copy.start()
        (early if k < 3 else loads).append(copy)
    conv_loads = [
        pltpu.make_async_copy(conv_hbm.at[:, dx], taps.at[dx], conv_sem.at[dx]) for dx in range(3)
    ]
    for load in conv_loads:
        load.start()
    pl.semaphore_wait(barrier, len(z_index) + len(xy_index))

    sends = []

    def send(src, dst, k, peer):
        copy = pltpu.make_async_remote_copy(
            src_ref=src, dst_ref=dst, send_sem=halo_send.at[k], recv_sem=halo_recv.at[k],
            device_id=peer, device_id_type=MESH,
        )
        copy.start()
        sends.append(copy)
        return copy

    rows = feat_hbm.at[0]
    from_left = send(rows.at[1], ext.at[1, 0], 0, (s, right))
    from_right = send(rows.at[0], ext.at[1, 3], 1, (s, left))
    from_down = send(rows, ext.at[0, pl.ds(1, 2)], 2, (up, q))
    from_up = send(rows, ext.at[2, pl.ds(1, 2)], 3, (down, q))

    def to_plane(buf, send_sem, recv_sem):
        for block in xy_index:
            pltpu.make_async_remote_copy(
                src_ref=buf.at[q], dst_ref=buf.at[q], send_sem=send_sem, recv_sem=recv_sem,
                device_id=(s, block), device_id_type=MESH,
            ).start()

    def wait_slots(buf, count, sem):
        some = buf.at[pl.ds(0, count)]
        pltpu.make_async_copy(some, some, sem).wait()

    for load in early:
        load.wait()
    qproj = (dot(qbuf[q].astype(BF16), wq[0]) * HEAD_DIM**-0.5).astype(BF16)
    qpbuf[q] = jnp.concatenate([qproj[:, 0:128], qproj[:, 128:256]], axis=0)
    to_plane(qpbuf, p_send, p_recv)

    perm = jnp.where(
        iota((D, D), 1) == (iota((D, D), 0) % HEAD_DIM) * HEADS + iota((D, D), 0) // HEAD_DIM, 1.0, 0.0
    ).astype(BF16)
    perm_t = jnp.where(
        iota((D, D), 0) == (iota((D, D), 1) % HEAD_DIM) * HEADS + iota((D, D), 1) // HEAD_DIM, 1.0, 0.0
    ).astype(BF16)
    for load in loads:
        load.wait()
    for layer in range(LAYERS):
        wvp[layer] = dot(wv[layer], perm).astype(BF16)
        wop[layer] = dot(perm_t, wo[layer]).astype(BF16)

    lists = mb[...]
    all_ids = lists.astype(F32).T.astype(jnp.int32)
    own_ids, picks, listed = [], [], []
    for r in range(2):
        block_id = s * NY + q * 2 + r
        listed.append(jnp.max(jnp.where(all_ids == block_id, 1, 0), axis=1, keepdims=True) > 0)
        picks.append(jnp.max(jnp.where(lists == block_id, 1.0, 0.0), axis=0, keepdims=True))
        own_ids.append(jnp.sum(jnp.where(listed[r], all_ids.astype(F32), 0.0), axis=0, keepdims=True))
    own_ids = jnp.concatenate(own_ids + [jnp.full((6, MB), -1.0, F32)], axis=0).astype(jnp.int32)
    picks = jnp.concatenate(picks + [jnp.zeros((6, NQ), F32)], axis=0).astype(BF16)

    col = iota((1, QRY * 32), 1)
    pair_id = slot_plane((col // 256) * 8 + col % 8, z) * NY + ((col % 256) // 16) * 2 + (col // 8) % 2
    row = iota((1, QRY * 16), 1)
    kind = row % 16
    term_y = jnp.where(kind < 6, (row // 16) * 2 + jnp.where(kind < 3, 0, 1), -1)
    lane_z = slot_plane(iota((1, 128), 1) // HEADS, z)

    from_left.wait_recv()
    send(ext.at[1, 0], ext.at[0, 0], 4, (up, q))
    send(ext.at[1, 0], ext.at[2, 0], 5, (down, q))
    from_right.wait_recv()
    send(ext.at[1, 3], ext.at[0, 3], 6, (up, q))
    send(ext.at[1, 3], ext.at[2, 3], 7, (down, q))
    own.wait()
    for load in conv_loads:
        load.wait()
    for copy in sends[2:]:
        copy.wait_recv()

    @pl.when(s == 0)
    def _():
        ext[0] = jnp.zeros((4, NX, D), BF16)

    @pl.when(s == SPAN - 1)
    def _():
        ext[2] = jnp.zeros((4, NX, D), BF16)

    for k in range(4, 8):
        sends[k].wait_send()

    @pl.when(q == 0)
    def _():
        ext[:, 0] = jnp.zeros((3, NX, D), BF16)

    @pl.when(q == QRY - 1)
    def _():
        ext[:, 3] = jnp.zeros((3, NX, D), BF16)

    slab = jnp.concatenate(
        [ext[dz, dy : dy + 2].reshape(2 * NX, D) for dz in range(3) for dy in range(3)], axis=1
    )
    x_at = iota((2 * NX, D), 0) % NX
    before = dot(slab, taps[0].reshape(9 * D, D))
    conv = jnp.where(x_at == 0, 0.0, pltpu.roll(before, 1, axis=0))
    conv = conv + dot(slab, taps[1].reshape(9 * D, D))
    after = dot(slab, taps[2].reshape(9 * D, D))
    conv = conv + jnp.where(x_at == NX - 1, 0.0, pltpu.roll(after, 2 * NX - 1, axis=0))
    pixel = jnp.maximum(conv, 0.0).astype(BF16)
    pix[...] = pixel
    keys[0] = dot(pixel, wk[0]).astype(BF16)
    vals[0] = dot(pixel, wvp[0]).astype(BF16)

    wait_slots(qpbuf, QRY - 1, p_recv)
    projected = jnp.concatenate(
        [qpbuf[:, half * 8 : half * 8 + 8, :].astype(F32).reshape(NQ, 128) for half in range(2)], axis=1
    )
    qproj = dot(picks, projected.astype(BF16))

    head_of = iota((HEADS, D), 1) // HEAD_DIM == iota((HEADS, D), 0)
    head_of_lane = iota((HEADS, D), 1) % HEADS == iota((HEADS, D), 0)
    lse_lane = iota((HEADS, 128), 1) % HEADS == iota((HEADS, 128), 0)
    own_slot = iota((HEADS, 128), 1) // HEADS
    for layer in range(LAYERS):
        spread = jnp.concatenate(
            [jnp.where(head_of, qproj[r : r + 1], 0.0) for r in range(2)], axis=0
        ).astype(BF16)
        scores = dot_nt(spread, keys[layer])
        scores = jnp.concatenate([scores[0:8, 0:NX], scores[8:16, NX : 2 * NX]], axis=0)
        top = jnp.max(scores, axis=1, keepdims=True)
        prob = jnp.exp(scores - top)
        total = jnp.sum(prob, axis=1, keepdims=True)
        inv = 1.0 / total
        lse = top + jnp.log(total)
        prob = prob.astype(BF16)
        low, high, lines = [], [], []
        for r in range(2):
            part = slice(r * HEADS, (r + 1) * HEADS)
            weighted = dot(prob[part], vals[layer, r * NX : (r + 1) * NX])
            out = jnp.sum(jnp.where(head_of_lane, weighted * inv[part], 0.0), axis=0, keepdims=True)
            low.append(out[:, 0:128])
            high.append(out[:, 128:256])
            lines.append(jnp.sum(jnp.where(lse_lane, lse[part], 0.0), axis=0, keepdims=True))
        buf = stage1.at[layer]
        buf[core] = jnp.concatenate(low + high + lines + [jnp.zeros((2, 128), F32)], axis=0)
        for (d, c), plane in zip(z_peers, z_index):
            place = Z_ORDER.index((ZS - d) % ZS)
            pltpu.make_async_remote_copy(
                src_ref=buf.at[core], dst_ref=buf.at[place * 2 + core],
                send_sem=s_send.at[layer], recv_sem=s_recv.at[layer, place // 4],
                device_id=(plane, q), device_id_type=MESH,
            ).start()
        if layer == 0:
            to_plane(qbuf, q_send, q_recv)
            keys[1] = dot(pix[...], wk[1]).astype(BF16)
            vals[1] = dot(pix[...], wvp[1]).astype(BF16)
        else:
            attn = merge(all_ids, near[0], far[0], pair_id, term_y, lane_z)
            state[...] = qbuf[...].reshape(NQ, D) + dot(attn.astype(BF16), wop[0])
        message, lines = [], []
        for group in range(2):
            wait_slots(buf, 7 + group, s_recv.at[layer, group])
            got = stage1[layer, group * 8 : group * 8 + 8]
            message = [got[:, k, :] for k in range(4)]
            lines.append(
                [
                    jnp.sum(
                        jnp.where(own_slot == group * 8 + iota((8, 128), 0), got[:, 4 + r, :], 0.0),
                        axis=0,
                        keepdims=True,
                    )
                    for r in range(2)
                ]
            )
            if group == 0:
                near[layer, q] = jnp.concatenate(message, axis=0).astype(BF16)
                to_plane(near.at[layer], y_send.at[layer, 0], y_recv.at[layer, 0])
        for r in range(2):
            line = lines[0][r] + lines[1][r]
            for _ in range(3):
                term = line.astype(BF16).astype(F32)
                message.append(term)
                line = line - term
        message.append(jnp.zeros((10, 128), F32))
        far[layer, q] = jnp.concatenate(message, axis=0).astype(BF16)
        to_plane(far.at[layer], y_send.at[layer, 1], y_recv.at[layer, 1])
        if layer == 0:
            wait_slots(qbuf, QRY - 1, q_recv)
            state_all = qbuf[...].reshape(NQ, D)
            own_state = [
                jnp.sum(jnp.where(listed[r], state_all, 0.0), axis=0, keepdims=True) for r in range(2)
            ]
            own_state = jnp.concatenate(own_state + [jnp.zeros((6, D), F32)], axis=0)
        wait_slots(near.at[layer], QRY - 1, y_recv.at[layer, 0])
        wait_slots(far.at[layer], QRY - 1, y_recv.at[layer, 1])
        if layer == 0:
            attn = merge(own_ids, near[0], far[0], pair_id, term_y, lane_z)
            own_state = own_state + dot(attn.astype(BF16), wop[0])
            qproj = (dot(own_state.astype(BF16), wq[1]) * HEAD_DIM**-0.5).astype(BF16).astype(F32)

    attn = merge(all_ids, near[1], far[1], pair_id, term_y, lane_z)
    final = state[...] + dot(attn.astype(BF16), wop[1])
    mean = jnp.mean(final, axis=-1, keepdims=True)
    centered = final - mean
    var = jnp.mean(centered * centered, axis=-1, keepdims=True)
    embed = centered * lax.rsqrt(var + 1e-05) * gain[...]
    state[...] = embed
    embed_ref[...] = state[pl.ds(pl.multiple_of(q * 8, 8), 8), :]
    mask_embed = dot(embed.astype(BF16), mw[...]).astype(BF16)
    logit_ref[...] = (dot_nt(mask_embed, pix[...]) * D**-0.5).astype(BF16)

    for copy in sends[:4]:
        copy.wait_send()
    wait_slots(qbuf, QRY - 1, q_send)
    wait_slots(qpbuf, QRY - 1, p_send)
    for layer in range(LAYERS):
        wait_slots(stage1.at[layer], SPAN - 1, s_send.at[layer])
        wait_slots(near.at[layer], QRY - 1, y_send.at[layer, 0])
        wait_slots(far.at[layer], QRY - 1, y_send.at[layer, 1])


def local(
    features, conv_weight, queries, w_query, w_key, w_value, w_out, norm_gain, mask_weight, mask_blocks
):
    hbm = pl.BlockSpec(memory_space=pltpu.HBM)
    vmem = pl.BlockSpec(memory_space=pltpu.VMEM)
    dma = pltpu.SemaphoreType.DMA
    square = pltpu.VMEM((LAYERS, D, D), BF16)
    embed, logits = pl.pallas_call(
        kernel,
        out_shape=(
            jax.ShapeDtypeStruct((8, D), F32),
            jax.ShapeDtypeStruct((NQ, 2 * NX), BF16),
        ),
        in_specs=[hbm] * 10,
        out_specs=(vmem, vmem),
        scratch_shapes=[
            pltpu.VMEM((3, 4, NX, D), BF16),
            pltpu.VMEM((3, 9, D, D), BF16),
            pltpu.VMEM((QRY, 8, D), F32),
            pltpu.VMEM((QRY, 16, 128), BF16),
            square,
            square,
            square,
            square,
            pltpu.VMEM((D, D), BF16),
            pltpu.VMEM((1, D), F32),
            pltpu.VMEM((MB, NQ), jnp.int32),
            square,
            square,
            pltpu.VMEM((2 * NX, D), BF16),
            square,
            square,
            pltpu.VMEM((LAYERS, SPAN, 8, 128), F32),
            pltpu.VMEM((LAYERS, QRY, NEAR_ROWS, 128), BF16),
            pltpu.VMEM((LAYERS, QRY, FAR_ROWS, 128), BF16),
            pltpu.VMEM((NQ, D), F32),
            dma((9,)),
            dma((3,)),
            dma((8,)),
            dma((8,)),
            dma,
            dma,
            dma,
            dma,
            dma((LAYERS,)),
            dma((LAYERS, 2)),
            dma((LAYERS, 2)),
            dma((LAYERS, 2)),
        ],
        compiler_params=pltpu.CompilerParams(
            collective_id=0, has_side_effects=True, vmem_limit_bytes=60 * 1024 * 1024
        ),
    )(
        features,
        conv_weight.reshape(9, 3, D, D),
        queries,
        w_query,
        w_key,
        w_value,
        w_out,
        norm_gain.reshape(1, D),
        mask_weight,
        mask_blocks.T,
    )
    return embed, logits.reshape(NQ, 1, 2, NX)


def solution(mesh):
    return jax.shard_map(
        local,
        mesh=mesh,
        in_specs=(
            P("span", "qry", None, None),
            P(),
            P("qry", None),
            P(),
            P(),
            P(),
            P(),
            P(),
            P(),
            P(),
        ),
        out_specs=(P("qry", None), P(None, "span", "qry", None)),
        check_vma=False,
    )
```

```python
import jax
import jax.numpy as jnp
from jax import lax
from jax.experimental import pallas as pl
from jax.experimental.pallas import tpu as pltpu
from jax.sharding import PartitionSpec as P

MESH = pl.DeviceIdType.MESH
HEADS = 8
LAYERS = 2
D = 256
HEAD_DIM = 32
NX = 128
NQ = 128
MB = 4
NY = 32
SPAN = 16
QRY = 16
F32 = jnp.float32
BF16 = jnp.bfloat16
ZS = 8
CHUNKS = 4
NEAR_ROWS = 32
FAR_ROWS = 48
Z_ORDER = (0, 1, 7, 2, 6, 3, 5, 4)
Z_SENDS = (4, 3, 5, 2, 6, 1, 7)
XY_SENDS = sorted(
    ((dy, dx) for dy in range(4) for dx in range(4) if dy or dx),
    key=lambda t: -(min(t[0], 4 - t[0]) + min(t[1], 4 - t[1])),
)


def iota(shape, dim):
    return lax.broadcasted_iota(jnp.int32, shape, dim)


def dot(a, b):
    return jnp.dot(a, b, preferred_element_type=F32)


def dot_nt(a, b):
    return lax.dot_general(a, b, (((1,), (1,)), ((), ())), preferred_element_type=F32)


def wrap(i, n):
    return lax.rem(i + n, n)


def slot_plane(slot, z):
    place = slot // 2
    offset = jnp.zeros_like(slot)
    for k, dz in enumerate(Z_ORDER):
        offset = jnp.where(place == k, dz, offset)
    return ((z + offset) % ZS) * 2 + slot % 2


def merge(ids, near, far, pair_id, term_y, lane_z):
    rows = ids.shape[0]
    outs = jnp.concatenate(
        [
            jnp.concatenate(
                [part[:, half * 16 : half * 16 + 16, :].reshape(QRY * 16, 128) for half in range(2)],
                axis=1,
            )
            for part in (near, far)
        ],
        axis=0,
    )
    terms = far[:, 32:FAR_ROWS, :].reshape(QRY * 16, 128)
    pick, term = [], []
    for j in range(MB):
        idj = ids[:, j : j + 1]
        pick.append(jnp.where(pair_id == idj, 1.0, 0.0).astype(BF16))
        term.append(jnp.where(term_y == idj % NY, 1.0, 0.0).astype(BF16))
    lse = dot(jnp.concatenate(term, axis=0), terms)
    chosen = dot(jnp.concatenate(pick, axis=0), outs)
    lses = []
    for j in range(MB):
        lj = jnp.where(lane_z == ids[:, j : j + 1] // NY, lse[j * rows : (j + 1) * rows], 0.0)
        for shift in (8, 16, 32, 64):
            lj = lj + pltpu.roll(lj, shift, axis=1)
        lses.append(lj)
    top = jnp.maximum(jnp.maximum(lses[0], lses[1]), jnp.maximum(lses[2], lses[3]))
    weights = [jnp.exp(lj - top) for lj in lses]
    inv = 1.0 / (weights[0] + weights[1] + weights[2] + weights[3])
    attn = jnp.zeros((rows, D), F32)
    for j in range(MB):
        wj = weights[j] * inv
        attn = attn + jnp.concatenate([wj, wj], axis=1) * chosen[j * rows : (j + 1) * rows]
    return attn


def kernel(
    feat_hbm, conv_hbm, queries_hbm, wq_hbm, wk_hbm, wv_hbm, wo_hbm, gain_hbm, mw_hbm, mb_hbm,
    embed_ref, logit_ref,
    ext, taps, qbuf, qpbuf, wq, wk, wv, wo, mw, gain, mb, wvp, wop, pix, keys, vals,
    stage1, near, far, state, acc,
    local_sem, conv_sem, halo_send, halo_recv, q_send, q_recv, p_send, p_recv,
    s_send, s_recv, y_send, y_recv,
):
    s = lax.axis_index("span")
    q = lax.axis_index("qry")
    z, core = s // 2, lax.rem(s, 2)
    y, x = q // 4, lax.rem(q, 4)
    up, down = wrap(s + 1, SPAN), wrap(s - 1, SPAN)
    right, left = wrap(q + 1, QRY), wrap(q - 1, QRY)
    z_peers = [(d, c) for d in Z_SENDS for c in range(2)] + [(0, 1)]
    z_index = [wrap(z + d, ZS) * 2 + (c if d else 1 - core) for d, c in z_peers]
    xy_index = [lax.rem(y + dy, 4) * 4 + lax.rem(x + dx, 4) for dy, dx in XY_SENDS]

    barrier = pltpu.get_barrier_semaphore()
    for plane in z_index[::-1]:
        pl.semaphore_signal(barrier, inc=1, device_id=(plane, q), device_id_type=MESH)
    for block in xy_index[::-1]:
        pl.semaphore_signal(barrier, inc=1, device_id=(s, block), device_id_type=MESH)

    own = pltpu.make_async_copy(feat_hbm.at[0], ext.at[1, pl.ds(1, 2)], local_sem.at[0])
    own.start()
    early, loads = [], []
    for k, (src, dst) in enumerate(
        (
            (mb_hbm, mb),
            (queries_hbm, qbuf.at[q]),
            (wq_hbm, wq),
            (wv_hbm, wv),
            (wo_hbm, wo),
            (wk_hbm, wk),
            (mw_hbm, mw),
            (gain_hbm, gain),
        )
    ):
        copy = pltpu.make_async_copy(src, dst, local_sem.at[1 + k])
        copy.start()
        (early if k < 3 else loads).append(copy)
    conv_loads = [
        pltpu.make_async_copy(conv_hbm.at[:, dx], taps.at[dx], conv_sem.at[dx]) for dx in range(3)
    ]
    for load in conv_loads:
        load.start()
    pl.semaphore_wait(barrier, len(z_index) + len(xy_index))

    sends = []

    def send(src, dst, k, peer):
        copy = pltpu.make_async_remote_copy(
            src_ref=src, dst_ref=dst, send_sem=halo_send.at[k], recv_sem=halo_recv.at[k],
            device_id=peer, device_id_type=MESH,
        )
        copy.start()
        sends.append(copy)
        return copy

    rows = feat_hbm.at[0]
    chunks = [pl.ds(k * (NX // CHUNKS), NX // CHUNKS) for k in range(CHUNKS)]
    across = []
    for k, chunk in enumerate(chunks):
        across.append(send(rows.at[1, chunk], ext.at[1, 0, chunk], 2 * k, (s, right)))
        across.append(send(rows.at[0, chunk], ext.at[1, 3, chunk], 2 * k + 1, (s, left)))
    from_down = send(rows, ext.at[0, pl.ds(1, 2)], 2 * CHUNKS, (up, q))
    from_up = send(rows, ext.at[2, pl.ds(1, 2)], 2 * CHUNKS + 1, (down, q))

    def to_plane(buf, send_sem, recv_sem):
        for block in xy_index:
            pltpu.make_async_remote_copy(
                src_ref=buf.at[q], dst_ref=buf.at[q], send_sem=send_sem, recv_sem=recv_sem,
                device_id=(s, block), device_id_type=MESH,
            ).start()

    def wait_slots(buf, count, sem):
        some = buf.at[pl.ds(0, count)]
        pltpu.make_async_copy(some, some, sem).wait()

    for load in early:
        load.wait()
    qproj = (dot(qbuf[q].astype(BF16), wq[0]) * HEAD_DIM**-0.5).astype(BF16)
    qpbuf[q] = jnp.concatenate([qproj[:, 0:128], qproj[:, 128:256]], axis=0)
    to_plane(qpbuf, p_send, p_recv)

    perm = jnp.where(
        iota((D, D), 1) == (iota((D, D), 0) % HEAD_DIM) * HEADS + iota((D, D), 0) // HEAD_DIM, 1.0, 0.0
    ).astype(BF16)
    perm_t = jnp.where(
        iota((D, D), 0) == (iota((D, D), 1) % HEAD_DIM) * HEADS + iota((D, D), 1) // HEAD_DIM, 1.0, 0.0
    ).astype(BF16)
    for load in loads:
        load.wait()
    for layer in range(LAYERS):
        wvp[layer] = dot(wv[layer], perm).astype(BF16)
        wop[layer] = dot(perm_t, wo[layer]).astype(BF16)

    lists = mb[...]
    all_ids = lists.astype(F32).T.astype(jnp.int32)
    own_ids, picks, listed = [], [], []
    for r in range(2):
        block_id = s * NY + q * 2 + r
        listed.append(jnp.max(jnp.where(all_ids == block_id, 1, 0), axis=1, keepdims=True) > 0)
        picks.append(jnp.max(jnp.where(lists == block_id, 1.0, 0.0), axis=0, keepdims=True))
        own_ids.append(jnp.sum(jnp.where(listed[r], all_ids.astype(F32), 0.0), axis=0, keepdims=True))
    own_ids = jnp.concatenate(own_ids + [jnp.full((6, MB), -1.0, F32)], axis=0).astype(jnp.int32)
    picks = jnp.concatenate(picks + [jnp.zeros((6, NQ), F32)], axis=0).astype(BF16)

    col = iota((1, QRY * 32), 1)
    pair_id = slot_plane((col // 256) * 8 + col % 8, z) * NY + ((col % 256) // 16) * 2 + (col // 8) % 2
    row = iota((1, QRY * 16), 1)
    kind = row % 16
    term_y = jnp.where(kind < 6, (row // 16) * 2 + jnp.where(kind < 3, 0, 1), -1)
    lane_z = slot_plane(iota((1, 128), 1) // HEADS, z)

    relays = []
    for k, copy in enumerate(across):
        copy.wait_recv()
        chunk, row = chunks[k // 2], 3 * (k % 2)
        first = 2 * CHUNKS + 2 + 2 * k
        relays.append(send(ext.at[1, row, chunk], ext.at[0, row, chunk], first, (up, q)))
        relays.append(send(ext.at[1, row, chunk], ext.at[2, row, chunk], first + 1, (down, q)))
    own.wait()
    for load in conv_loads:
        load.wait()

    middle = [ext[1, row] for row in range(4)]
    middle[0] = jnp.where(q > 0, middle[0], jnp.zeros_like(middle[0]))
    middle[3] = jnp.where(q < QRY - 1, middle[3], jnp.zeros_like(middle[3]))
    slab = jnp.concatenate(
        [jnp.concatenate(middle[dy : dy + 2], axis=0) for dy in range(3)], axis=1
    )
    for dx in range(3):
        acc[dx] = dot(slab, taps[dx, 3:6].reshape(3 * D, D))
    for dz, copy, outside in ((0, from_down, s == 0), (2, from_up, s == SPAN - 1)):
        copy.wait_recv()

        @pl.when(outside)
        def _():
            ext[dz, 1:3] = jnp.zeros((2, NX, D), BF16)

        pair = jnp.concatenate([ext[dz, 1], ext[dz, 2]], axis=1)
        for dx in range(3):
            for r in range(2):
                weights = taps[dx, 3 * dz + 1 - r : 3 * dz + 3 - r].reshape(2 * D, D)
                acc[dx, r * NX : (r + 1) * NX] += dot(pair, weights)

    for copy in relays:
        copy.wait_recv()

    @pl.when((s == 0) | (q == 0))
    def _():
        ext[0, 0] = jnp.zeros((NX, D), BF16)

    @pl.when((s == 0) | (q == QRY - 1))
    def _():
        ext[0, 3] = jnp.zeros((NX, D), BF16)

    @pl.when((s == SPAN - 1) | (q == 0))
    def _():
        ext[2, 0] = jnp.zeros((NX, D), BF16)

    @pl.when((s == SPAN - 1) | (q == QRY - 1))
    def _():
        ext[2, 3] = jnp.zeros((NX, D), BF16)

    def column(dx):
        parts = []
        for r in range(2):
            corner = jnp.concatenate([ext[0, 3 * r], ext[2, 3 * r]], axis=1)
            weights = jnp.concatenate([taps[dx, 2 * r], taps[dx, 6 + 2 * r]], axis=0)
            parts.append(acc[dx, r * NX : (r + 1) * NX] + dot(corner, weights))
        return jnp.concatenate(parts, axis=0)

    x_at = iota((2 * NX, D), 0) % NX
    conv = jnp.where(x_at == 0, 0.0, pltpu.roll(column(0), 1, axis=0))
    conv = conv + column(1)
    conv = conv + jnp.where(x_at == NX - 1, 0.0, pltpu.roll(column(2), 2 * NX - 1, axis=0))
    pixel = jnp.maximum(conv, 0.0).astype(BF16)
    pix[...] = pixel
    keys[0] = dot(pixel, wk[0]).astype(BF16)
    vals[0] = dot(pixel, wvp[0]).astype(BF16)

    wait_slots(qpbuf, QRY - 1, p_recv)
    projected = jnp.concatenate(
        [qpbuf[:, half * 8 : half * 8 + 8, :].astype(F32).reshape(NQ, 128) for half in range(2)], axis=1
    )
    qproj = dot(picks, projected.astype(BF16))

    head_of = iota((HEADS, D), 1) // HEAD_DIM == iota((HEADS, D), 0)
    head_of_lane = iota((HEADS, D), 1) % HEADS == iota((HEADS, D), 0)
    lse_lane = iota((HEADS, 128), 1) % HEADS == iota((HEADS, 128), 0)
    own_slot = iota((HEADS, 128), 1) // HEADS
    for layer in range(LAYERS):
        spread = jnp.concatenate(
            [jnp.where(head_of, qproj[r : r + 1], 0.0) for r in range(2)], axis=0
        ).astype(BF16)
        scores = dot_nt(spread, keys[layer])
        scores = jnp.concatenate([scores[0:8, 0:NX], scores[8:16, NX : 2 * NX]], axis=0)
        top = jnp.max(scores, axis=1, keepdims=True)
        prob = jnp.exp(scores - top)
        total = jnp.sum(prob, axis=1, keepdims=True)
        inv = 1.0 / total
        lse = top + jnp.log(total)
        prob = prob.astype(BF16)
        low, high, lines = [], [], []
        for r in range(2):
            part = slice(r * HEADS, (r + 1) * HEADS)
            weighted = dot(prob[part], vals[layer, r * NX : (r + 1) * NX])
            out = jnp.sum(jnp.where(head_of_lane, weighted * inv[part], 0.0), axis=0, keepdims=True)
            low.append(out[:, 0:128])
            high.append(out[:, 128:256])
            lines.append(jnp.sum(jnp.where(lse_lane, lse[part], 0.0), axis=0, keepdims=True))
        buf = stage1.at[layer]
        buf[core] = jnp.concatenate(low + high + lines + [jnp.zeros((2, 128), F32)], axis=0)
        for (d, c), plane in zip(z_peers, z_index):
            place = Z_ORDER.index((ZS - d) % ZS)
            pltpu.make_async_remote_copy(
                src_ref=buf.at[core], dst_ref=buf.at[place * 2 + core],
                send_sem=s_send.at[layer], recv_sem=s_recv.at[layer, place // 4],
                device_id=(plane, q), device_id_type=MESH,
            ).start()
        if layer == 0:
            to_plane(qbuf, q_send, q_recv)
            keys[1] = dot(pix[...], wk[1]).astype(BF16)
            vals[1] = dot(pix[...], wvp[1]).astype(BF16)
        else:
            attn = merge(all_ids, near[0], far[0], pair_id, term_y, lane_z)
            state[...] = qbuf[...].reshape(NQ, D) + dot(attn.astype(BF16), wop[0])
        message, lines = [], []
        for group in range(2):
            wait_slots(buf, 7 + group, s_recv.at[layer, group])
            got = stage1[layer, group * 8 : group * 8 + 8]
            message = [got[:, k, :] for k in range(4)]
            lines.append(
                [
                    jnp.sum(
                        jnp.where(own_slot == group * 8 + iota((8, 128), 0), got[:, 4 + r, :], 0.0),
                        axis=0,
                        keepdims=True,
                    )
                    for r in range(2)
                ]
            )
            if group == 0:
                near[layer, q] = jnp.concatenate(message, axis=0).astype(BF16)
                to_plane(near.at[layer], y_send.at[layer, 0], y_recv.at[layer, 0])
        for r in range(2):
            line = lines[0][r] + lines[1][r]
            for _ in range(3):
                term = line.astype(BF16).astype(F32)
                message.append(term)
                line = line - term
        message.append(jnp.zeros((10, 128), F32))
        far[layer, q] = jnp.concatenate(message, axis=0).astype(BF16)
        to_plane(far.at[layer], y_send.at[layer, 1], y_recv.at[layer, 1])
        if layer == 0:
            wait_slots(qbuf, QRY - 1, q_recv)
            state_all = qbuf[...].reshape(NQ, D)
            own_state = [
                jnp.sum(jnp.where(listed[r], state_all, 0.0), axis=0, keepdims=True) for r in range(2)
            ]
            own_state = jnp.concatenate(own_state + [jnp.zeros((6, D), F32)], axis=0)
        wait_slots(near.at[layer], QRY - 1, y_recv.at[layer, 0])
        wait_slots(far.at[layer], QRY - 1, y_recv.at[layer, 1])
        if layer == 0:
            attn = merge(own_ids, near[0], far[0], pair_id, term_y, lane_z)
            own_state = own_state + dot(attn.astype(BF16), wop[0])
            qproj = (dot(own_state.astype(BF16), wq[1]) * HEAD_DIM**-0.5).astype(BF16).astype(F32)

    attn = merge(all_ids, near[1], far[1], pair_id, term_y, lane_z)
    final = state[...] + dot(attn.astype(BF16), wop[1])
    mean = jnp.mean(final, axis=-1, keepdims=True)
    centered = final - mean
    var = jnp.mean(centered * centered, axis=-1, keepdims=True)
    embed = centered * lax.rsqrt(var + 1e-05) * gain[...]
    state[...] = embed
    embed_ref[...] = state[pl.ds(pl.multiple_of(q * 8, 8), 8), :]
    mask_embed = dot(embed.astype(BF16), mw[...]).astype(BF16)
    logit_ref[...] = (dot_nt(mask_embed, pix[...]) * D**-0.5).astype(BF16)

    for copy in sends:
        copy.wait_send()
    wait_slots(qbuf, QRY - 1, q_send)
    wait_slots(qpbuf, QRY - 1, p_send)
    for layer in range(LAYERS):
        wait_slots(stage1.at[layer], SPAN - 1, s_send.at[layer])
        wait_slots(near.at[layer], QRY - 1, y_send.at[layer, 0])
        wait_slots(far.at[layer], QRY - 1, y_send.at[layer, 1])


def local(
    features, conv_weight, queries, w_query, w_key, w_value, w_out, norm_gain, mask_weight, mask_blocks
):
    hbm = pl.BlockSpec(memory_space=pltpu.HBM)
    vmem = pl.BlockSpec(memory_space=pltpu.VMEM)
    dma = pltpu.SemaphoreType.DMA
    square = pltpu.VMEM((LAYERS, D, D), BF16)
    embed, logits = pl.pallas_call(
        kernel,
        out_shape=(
            jax.ShapeDtypeStruct((8, D), F32),
            jax.ShapeDtypeStruct((NQ, 2 * NX), BF16),
        ),
        in_specs=[hbm] * 10,
        out_specs=(vmem, vmem),
        scratch_shapes=[
            pltpu.VMEM((3, 4, NX, D), BF16),
            pltpu.VMEM((3, 9, D, D), BF16),
            pltpu.VMEM((QRY, 8, D), F32),
            pltpu.VMEM((QRY, 16, 128), BF16),
            square,
            square,
            square,
            square,
            pltpu.VMEM((D, D), BF16),
            pltpu.VMEM((1, D), F32),
            pltpu.VMEM((MB, NQ), jnp.int32),
            square,
            square,
            pltpu.VMEM((2 * NX, D), BF16),
            square,
            square,
            pltpu.VMEM((LAYERS, SPAN, 8, 128), F32),
            pltpu.VMEM((LAYERS, QRY, NEAR_ROWS, 128), BF16),
            pltpu.VMEM((LAYERS, QRY, FAR_ROWS, 128), BF16),
            pltpu.VMEM((NQ, D), F32),
            pltpu.VMEM((3, 2 * NX, D), F32),
            dma((9,)),
            dma((3,)),
            dma((6 * CHUNKS + 2,)),
            dma((6 * CHUNKS + 2,)),
            dma,
            dma,
            dma,
            dma,
            dma((LAYERS,)),
            dma((LAYERS, 2)),
            dma((LAYERS, 2)),
            dma((LAYERS, 2)),
        ],
        compiler_params=pltpu.CompilerParams(
            collective_id=0, has_side_effects=True, vmem_limit_bytes=60 * 1024 * 1024
        ),
    )(
        features,
        conv_weight.reshape(9, 3, D, D),
        queries,
        w_query,
        w_key,
        w_value,
        w_out,
        norm_gain.reshape(1, D),
        mask_weight,
        mask_blocks.T,
    )
    return embed, logits.reshape(NQ, 1, 2, NX)


def solution(mesh):
    return jax.shard_map(
        local,
        mesh=mesh,
        in_specs=(
            P("span", "qry", None, None),
            P(),
            P("qry", None),
            P(),
            P(),
            P(),
            P(),
            P(),
            P(),
            P(),
        ),
        out_specs=(P("qry", None), P(None, "span", "qry", None)),
        check_vma=False,
    )
```

```python
import jax
import jax.numpy as jnp
from jax import lax
from jax.experimental import pallas as pl
from jax.experimental.pallas import tpu as pltpu
from jax.sharding import PartitionSpec as P

MESH = pl.DeviceIdType.MESH
HEADS = 8
LAYERS = 2
D = 256
HEAD_DIM = 32
NX = 128
NQ = 128
MB = 4
NY = 32
SPAN = 16
QRY = 16
F32 = jnp.float32
BF16 = jnp.bfloat16
ZS = 8
CHUNKS = 4
Z_ORDER = (0, 1, 7, 2, 6, 3, 5, 4)
GROUPS = ((0, 8), (8, 14), (14, 16))
PLACE_GROUP = (0, 0, 0, 0, 1, 1, 1, 2)
Z_SENDS = (4, 3, 5, 2, 6, 1, 7)
XY_SENDS = sorted(
    ((dy, dx) for dy in range(4) for dx in range(4) if dy or dx),
    key=lambda t: -(min(t[0], 4 - t[0]) + min(t[1], 4 - t[1])),
)


def iota(shape, dim):
    return lax.broadcasted_iota(jnp.int32, shape, dim)


def dot(a, b):
    return jnp.dot(a, b, preferred_element_type=F32)


def dot_nt(a, b):
    return lax.dot_general(a, b, (((1,), (1,)), ((), ())), preferred_element_type=F32)


def wrap(i, n):
    return lax.rem(i + n, n)


def slot_plane(slot, z):
    place = slot // 2
    offset = jnp.zeros_like(slot)
    for k, dz in enumerate(Z_ORDER):
        offset = jnp.where(place == k, dz, offset)
    return ((z + offset) % ZS) * 2 + slot % 2


def merge(ids, near, mid, far, pair_id, term_y, lane_z):
    rows = ids.shape[0]
    flat = far.reshape(QRY * 16, 128)
    raised = pltpu.roll(flat.astype(F32), QRY * 16 - 4, axis=0).astype(BF16)
    outs = jnp.concatenate(
        [
            jnp.concatenate([near[half].reshape(QRY * 16, 128) for half in range(2)], axis=1),
            jnp.concatenate(
                [mid[:, half * 16 : half * 16 + 16, :].reshape(QRY * 16, 128) for half in range(2)],
                axis=1,
            ),
            jnp.concatenate([flat, raised], axis=1),
        ],
        axis=0,
    )
    pick, term = [], []
    for j in range(MB):
        idj = ids[:, j : j + 1]
        pick.append(jnp.where(pair_id == idj, 1.0, 0.0).astype(BF16))
        term.append(jnp.where(term_y == idj % NY, 1.0, 0.0).astype(BF16))
    lse = dot(jnp.concatenate(term, axis=0), flat)
    chosen = dot(jnp.concatenate(pick, axis=0), outs)
    lses = []
    for j in range(MB):
        lj = jnp.where(lane_z == ids[:, j : j + 1] // NY, lse[j * rows : (j + 1) * rows], 0.0)
        for shift in (8, 16, 32, 64):
            lj = lj + pltpu.roll(lj, shift, axis=1)
        lses.append(lj)
    top = jnp.maximum(jnp.maximum(lses[0], lses[1]), jnp.maximum(lses[2], lses[3]))
    weights = [jnp.exp(lj - top) for lj in lses]
    inv = 1.0 / (weights[0] + weights[1] + weights[2] + weights[3])
    attn = jnp.zeros((rows, D), F32)
    for j in range(MB):
        wj = weights[j] * inv
        attn = attn + jnp.concatenate([wj, wj], axis=1) * chosen[j * rows : (j + 1) * rows]
    return attn


def kernel(
    feat_hbm, conv_hbm, queries_hbm, wq_hbm, wk_hbm, wv_hbm, wo_hbm, gain_hbm, mw_hbm, mb_hbm,
    embed_ref, logit_ref,
    ext, taps, qbuf, qpbuf, wq, wk, wv, wo, mw, gain, mb, wvp, wop, pix, keys, vals,
    stage1, near, mid, far, state, acc,
    local_sem, conv_sem, halo_send, halo_recv, q_send, q_recv, p_send, p_recv,
    s_send, s_recv, y_send, y_recv, c_send, c_recv, entered,
):
    s = lax.axis_index("span")
    q = lax.axis_index("qry")
    z, core = s // 2, lax.rem(s, 2)
    y, x = q // 4, lax.rem(q, 4)
    up, down = wrap(s + 1, SPAN), wrap(s - 1, SPAN)
    right, left = wrap(q + 1, QRY), wrap(q - 1, QRY)
    z_peers = [(d, c) for d in Z_SENDS for c in range(2)] + [(0, 1)]
    z_index = [wrap(z + d, ZS) * 2 + (c if d else 1 - core) for d, c in z_peers]
    xy_index = [lax.rem(y + dy, 4) * 4 + lax.rem(x + dx, 4) for dy, dx in XY_SENDS]

    barrier = pltpu.get_barrier_semaphore()
    for d in (1, -1, 2, -2):
        pl.semaphore_signal(barrier, inc=1, device_id=(wrap(s + d, SPAN), q), device_id_type=MESH)
    for block in xy_index[::-1]:
        pl.semaphore_signal(barrier, inc=1, device_id=(s, block), device_id_type=MESH)

    own = pltpu.make_async_copy(feat_hbm.at[0], ext.at[1, pl.ds(1, 2)], local_sem.at[0])
    own.start()
    early, loads = [], []
    for k, (src, dst) in enumerate(
        (
            (mb_hbm, mb),
            (queries_hbm, qbuf.at[q]),
            (wq_hbm, wq),
            (wv_hbm, wv),
            (wo_hbm, wo),
            (wk_hbm, wk),
            (mw_hbm, mw),
            (gain_hbm, gain),
        )
    ):
        copy = pltpu.make_async_copy(src, dst, local_sem.at[1 + k])
        copy.start()
        (early if k < 3 else loads).append(copy)
    conv_loads = [
        pltpu.make_async_copy(conv_hbm.at[:, dx], taps.at[dx], conv_sem.at[dx]) for dx in range(3)
    ]
    for load in conv_loads:
        load.start()
    pl.semaphore_wait(barrier, 4 + len(xy_index))

    def tell(step):
        for k, d in enumerate((2 * step, -2 * step)):
            pl.semaphore_signal(
                entered.at[step - 1, k], inc=1, device_id=(wrap(s + d, SPAN), q), device_id_type=MESH
            )

    def hear(step):
        for k in range(2):
            pl.semaphore_wait(entered.at[step - 1, k], 1)

    sends = []

    def send(src, dst, k, peer):
        copy = pltpu.make_async_remote_copy(
            src_ref=src, dst_ref=dst, send_sem=halo_send.at[k], recv_sem=halo_recv.at[k],
            device_id=peer, device_id_type=MESH,
        )
        copy.start()
        sends.append(copy)
        return copy

    rows = feat_hbm.at[0]
    chunks = [pl.ds(k * (NX // CHUNKS), NX // CHUNKS) for k in range(CHUNKS)]
    across = []
    for k, chunk in enumerate(chunks):
        across.append(send(rows.at[1, chunk], ext.at[1, 0, chunk], 2 * k, (s, right)))
        across.append(send(rows.at[0, chunk], ext.at[1, 3, chunk], 2 * k + 1, (s, left)))
    from_down = send(rows, ext.at[0, pl.ds(1, 2)], 2 * CHUNKS, (up, q))
    from_up = send(rows, ext.at[2, pl.ds(1, 2)], 2 * CHUNKS + 1, (down, q))

    tell(1)

    def to_plane(buf, send_sem, recv_sem):
        for block in xy_index:
            pltpu.make_async_remote_copy(
                src_ref=buf.at[q], dst_ref=buf.at[q], send_sem=send_sem, recv_sem=recv_sem,
                device_id=(s, block), device_id_type=MESH,
            ).start()

    def wait_slots(buf, count, sem):
        some = buf.at[pl.ds(0, count)]
        pltpu.make_async_copy(some, some, sem).wait()

    for load in early:
        load.wait()
    qproj = (dot(qbuf[q].astype(BF16), wq[0]) * HEAD_DIM**-0.5).astype(BF16)
    qpbuf[q] = jnp.concatenate([qproj[:, 0:128], qproj[:, 128:256]], axis=0)
    to_plane(qpbuf, p_send, p_recv)

    perm = jnp.where(
        iota((D, D), 1) == (iota((D, D), 0) % HEAD_DIM) * HEADS + iota((D, D), 0) // HEAD_DIM, 1.0, 0.0
    ).astype(BF16)
    perm_t = jnp.where(
        iota((D, D), 0) == (iota((D, D), 1) % HEAD_DIM) * HEADS + iota((D, D), 1) // HEAD_DIM, 1.0, 0.0
    ).astype(BF16)
    for load in loads:
        load.wait()
    for layer in range(LAYERS):
        wvp[layer] = dot(wv[layer], perm).astype(BF16)
        wop[layer] = dot(perm_t, wo[layer]).astype(BF16)

    lists = mb[...]
    all_ids = lists.astype(F32).T.astype(jnp.int32)
    own_ids, picks, listed = [], [], []
    for r in range(2):
        block_id = s * NY + q * 2 + r
        listed.append(jnp.max(jnp.where(all_ids == block_id, 1, 0), axis=1, keepdims=True) > 0)
        picks.append(jnp.max(jnp.where(lists == block_id, 1.0, 0.0), axis=0, keepdims=True))
        own_ids.append(jnp.sum(jnp.where(listed[r], all_ids.astype(F32), 0.0), axis=0, keepdims=True))
    own_ids = jnp.concatenate(own_ids + [jnp.full((6, MB), -1.0, F32)], axis=0).astype(jnp.int32)
    picks = jnp.concatenate(picks + [jnp.zeros((6, NQ), F32)], axis=0).astype(BF16)

    col = iota((1, QRY * 48), 1)
    group, kind = col // 256, col % 16
    slot = jnp.where(group < 2, group * 8 + col % 8, 14 + col % 2)
    half = jnp.where(group < 2, kind // 8, kind // 2)
    limit = jnp.where(group == 0, 8, jnp.where(group == 1, 6, 4))
    pair_id = slot_plane(slot, z) * NY + ((col % 256) // 16) * 2 + half
    pair_id = jnp.where(jnp.where(group < 2, col % 8, kind) < limit, pair_id, -2)
    row = iota((1, QRY * 16), 1)
    kind = row % 16 - 8
    term_y = (row // 16) * 2 + jnp.where(kind < 3, 0, 1)
    term_y = jnp.where((kind >= 0) & (kind < 6), term_y, -2)
    lane_z = slot_plane(iota((1, 128), 1) // HEADS, z)

    relays = []
    for k, copy in enumerate(across):
        copy.wait_recv()
        chunk, row = chunks[k // 2], 3 * (k % 2)
        first = 2 * CHUNKS + 2 + 2 * k
        relays.append(send(ext.at[1, row, chunk], ext.at[0, row, chunk], first, (up, q)))
        relays.append(send(ext.at[1, row, chunk], ext.at[2, row, chunk], first + 1, (down, q)))
    hear(1)
    tell(2)
    own.wait()
    for load in conv_loads:
        load.wait()

    middle = [ext[1, row] for row in range(4)]
    middle[0] = jnp.where(q > 0, middle[0], jnp.zeros_like(middle[0]))
    middle[3] = jnp.where(q < QRY - 1, middle[3], jnp.zeros_like(middle[3]))
    slab = jnp.concatenate(
        [jnp.concatenate(middle[dy : dy + 2], axis=0) for dy in range(3)], axis=1
    )
    for dx in range(3):
        acc[dx] = dot(slab, taps[dx, 3:6].reshape(3 * D, D))
    for dz, copy, outside in ((0, from_down, s == 0), (2, from_up, s == SPAN - 1)):
        copy.wait_recv()

        @pl.when(outside)
        def _():
            ext[dz, 1:3] = jnp.zeros((2, NX, D), BF16)

        pair = jnp.concatenate([ext[dz, 1], ext[dz, 2]], axis=1)
        for dx in range(3):
            for r in range(2):
                weights = taps[dx, 3 * dz + 1 - r : 3 * dz + 3 - r].reshape(2 * D, D)
                acc[dx, r * NX : (r + 1) * NX] += dot(pair, weights)

    for copy in relays:
        copy.wait_recv()

    @pl.when((s == 0) | (q == 0))
    def _():
        ext[0, 0] = jnp.zeros((NX, D), BF16)

    @pl.when((s == 0) | (q == QRY - 1))
    def _():
        ext[0, 3] = jnp.zeros((NX, D), BF16)

    @pl.when((s == SPAN - 1) | (q == 0))
    def _():
        ext[2, 0] = jnp.zeros((NX, D), BF16)

    @pl.when((s == SPAN - 1) | (q == QRY - 1))
    def _():
        ext[2, 3] = jnp.zeros((NX, D), BF16)

    def column(dx):
        parts = []
        for r in range(2):
            corner = jnp.concatenate([ext[0, 3 * r], ext[2, 3 * r]], axis=1)
            weights = jnp.concatenate([taps[dx, 2 * r], taps[dx, 6 + 2 * r]], axis=0)
            parts.append(acc[dx, r * NX : (r + 1) * NX] + dot(corner, weights))
        return jnp.concatenate(parts, axis=0)

    x_at = iota((2 * NX, D), 0) % NX
    conv = jnp.where(x_at == 0, 0.0, pltpu.roll(column(0), 1, axis=0))
    conv = conv + column(1)
    conv = conv + jnp.where(x_at == NX - 1, 0.0, pltpu.roll(column(2), 2 * NX - 1, axis=0))
    pixel = jnp.maximum(conv, 0.0).astype(BF16)
    pix[...] = pixel
    keys[0] = dot(pixel, wk[0]).astype(BF16)
    vals[0] = dot(pixel, wvp[0]).astype(BF16)

    wait_slots(qpbuf, QRY - 1, p_recv)
    projected = jnp.concatenate(
        [qpbuf[:, half * 8 : half * 8 + 8, :].astype(F32).reshape(NQ, 128) for half in range(2)], axis=1
    )
    qproj = dot(picks, projected.astype(BF16))

    head_of = iota((HEADS, D), 1) // HEAD_DIM == iota((HEADS, D), 0)
    head_of_lane = iota((HEADS, D), 1) % HEADS == iota((HEADS, D), 0)
    lse_lane = iota((HEADS, 128), 1) % HEADS == iota((HEADS, 128), 0)
    hear(2)
    for layer in range(LAYERS):
        spread = jnp.concatenate(
            [jnp.where(head_of, qproj[r : r + 1], 0.0) for r in range(2)], axis=0
        ).astype(BF16)
        scores = dot_nt(spread, keys[layer])
        scores = jnp.concatenate([scores[0:8, 0:NX], scores[8:16, NX : 2 * NX]], axis=0)
        top = jnp.max(scores, axis=1, keepdims=True)
        prob = jnp.exp(scores - top)
        total = jnp.sum(prob, axis=1, keepdims=True)
        inv = 1.0 / total
        lse = top + jnp.log(total)
        prob = prob.astype(BF16)
        low, high, lines = [], [], []
        for r in range(2):
            part = slice(r * HEADS, (r + 1) * HEADS)
            weighted = dot(prob[part], vals[layer, r * NX : (r + 1) * NX])
            out = jnp.sum(jnp.where(head_of_lane, weighted * inv[part], 0.0), axis=0, keepdims=True)
            low.append(out[:, 0:128])
            high.append(out[:, 128:256])
            lines.append(jnp.sum(jnp.where(lse_lane, lse[part], 0.0), axis=0, keepdims=True))
        buf = stage1.at[layer]
        buf[core] = jnp.concatenate(low + high + lines + [jnp.zeros((2, 128), F32)], axis=0)
        for (d, c), plane in zip(z_peers, z_index):
            place = Z_ORDER.index((ZS - d) % ZS)
            pltpu.make_async_remote_copy(
                src_ref=buf.at[core], dst_ref=buf.at[place * 2 + core],
                send_sem=s_send.at[layer], recv_sem=s_recv.at[layer, PLACE_GROUP[place]],
                device_id=(plane, q), device_id_type=MESH,
            ).start()
        if layer == 0:
            to_plane(qbuf, q_send, q_recv)
            keys[1] = dot(pix[...], wk[1]).astype(BF16)
            vals[1] = dot(pix[...], wvp[1]).astype(BF16)
        else:
            attn = merge(all_ids, near[0], mid[0], far[0], pair_id, term_y, lane_z)
            state[...] = qbuf[...].reshape(NQ, D) + dot(attn.astype(BF16), wop[0])
        lines = [jnp.zeros((1, 128), F32)] * 2
        for group, (start, end) in enumerate(GROUPS):
            count = end - start
            wait_slots(buf, count - (group == 0), s_recv.at[layer, group])
            got = stage1[layer, start:end]
            parts = [got[:, k, :] for k in range(4)]
            own_lanes = iota((count, 128), 1) // HEADS == start + iota((count, 128), 0)
            for r in range(2):
                kept = jnp.where(own_lanes, got[:, 4 + r, :], 0.0)
                lines[r] = lines[r] + jnp.sum(kept, axis=0, keepdims=True)
            if group == 0:
                halves = [jnp.concatenate(parts[2 * k : 2 * k + 2], axis=0) for k in range(2)]
                near[layer, core, q] = jnp.where(core == 0, halves[0], halves[1]).astype(BF16)
                to_plane(near.at[layer, core], y_send.at[layer, 0], y_recv.at[layer, 0])
            elif group == 1:
                blank = jnp.zeros((2, 128), F32)
                message = [piece for part in parts for piece in (part, blank)]
                mid[layer, q] = jnp.concatenate(message, axis=0).astype(BF16)
                to_plane(mid.at[layer], y_send.at[layer, 1], y_recv.at[layer, 1])
        message = parts
        for line in lines:
            for _ in range(3):
                term = line.astype(BF16).astype(F32)
                message.append(term)
                line = line - term
        message.append(jnp.zeros((2, 128), F32))
        far[layer, q] = jnp.concatenate(message, axis=0).astype(BF16)
        to_plane(far.at[layer], y_send.at[layer, 2], y_recv.at[layer, 2])
        if layer == 0:
            wait_slots(qbuf, QRY - 1, q_recv)
            state_all = qbuf[...].reshape(NQ, D)
            own_state = [
                jnp.sum(jnp.where(listed[r], state_all, 0.0), axis=0, keepdims=True) for r in range(2)
            ]
            own_state = jnp.concatenate(own_state + [jnp.zeros((6, D), F32)], axis=0)
        wait_slots(near.at[layer, 0], QRY - 1, y_recv.at[layer, 0])
        swap = pltpu.make_async_remote_copy(
            src_ref=near.at[layer, core], dst_ref=near.at[layer, core],
            send_sem=c_send.at[layer], recv_sem=c_recv.at[layer],
            device_id=(z * 2 + 1 - core, q), device_id_type=MESH,
        )
        swap.start()
        sends.append(swap)
        wait_slots(mid.at[layer], QRY - 1, y_recv.at[layer, 1])
        wait_slots(far.at[layer], QRY - 1, y_recv.at[layer, 2])
        swap.wait_recv()
        if layer == 0:
            attn = merge(own_ids, near[0], mid[0], far[0], pair_id, term_y, lane_z)
            own_state = own_state + dot(attn.astype(BF16), wop[0])
            qproj = (dot(own_state.astype(BF16), wq[1]) * HEAD_DIM**-0.5).astype(BF16).astype(F32)

    attn = merge(all_ids, near[1], mid[1], far[1], pair_id, term_y, lane_z)
    final = state[...] + dot(attn.astype(BF16), wop[1])
    mean = jnp.mean(final, axis=-1, keepdims=True)
    centered = final - mean
    var = jnp.mean(centered * centered, axis=-1, keepdims=True)
    embed = centered * lax.rsqrt(var + 1e-05) * gain[...]
    state[...] = embed
    embed_ref[...] = state[pl.ds(pl.multiple_of(q * 8, 8), 8), :]
    mask_embed = dot(embed.astype(BF16), mw[...]).astype(BF16)
    logit_ref[...] = (dot_nt(mask_embed, pix[...]) * D**-0.5).astype(BF16)

    for copy in sends:
        copy.wait_send()
    wait_slots(qbuf, QRY - 1, q_send)
    wait_slots(qpbuf, QRY - 1, p_send)
    for layer in range(LAYERS):
        wait_slots(stage1.at[layer], SPAN - 1, s_send.at[layer])
        wait_slots(near.at[layer, 0], QRY - 1, y_send.at[layer, 0])
        wait_slots(mid.at[layer], QRY - 1, y_send.at[layer, 1])
        wait_slots(far.at[layer], QRY - 1, y_send.at[layer, 2])


def local(
    features, conv_weight, queries, w_query, w_key, w_value, w_out, norm_gain, mask_weight, mask_blocks
):
    hbm = pl.BlockSpec(memory_space=pltpu.HBM)
    vmem = pl.BlockSpec(memory_space=pltpu.VMEM)
    dma = pltpu.SemaphoreType.DMA
    square = pltpu.VMEM((LAYERS, D, D), BF16)
    embed, logits = pl.pallas_call(
        kernel,
        out_shape=(
            jax.ShapeDtypeStruct((8, D), F32),
            jax.ShapeDtypeStruct((NQ, 2 * NX), BF16),
        ),
        in_specs=[hbm] * 10,
        out_specs=(vmem, vmem),
        scratch_shapes=[
            pltpu.VMEM((3, 4, NX, D), BF16),
            pltpu.VMEM((3, 9, D, D), BF16),
            pltpu.VMEM((QRY, 8, D), F32),
            pltpu.VMEM((QRY, 16, 128), BF16),
            square,
            square,
            square,
            square,
            pltpu.VMEM((D, D), BF16),
            pltpu.VMEM((1, D), F32),
            pltpu.VMEM((MB, NQ), jnp.int32),
            square,
            square,
            pltpu.VMEM((2 * NX, D), BF16),
            square,
            square,
            pltpu.VMEM((LAYERS, SPAN, 8, 128), F32),
            pltpu.VMEM((LAYERS, 2, QRY, 16, 128), BF16),
            pltpu.VMEM((LAYERS, QRY, 32, 128), BF16),
            pltpu.VMEM((LAYERS, QRY, 16, 128), BF16),
            pltpu.VMEM((NQ, D), F32),
            pltpu.VMEM((3, 2 * NX, D), F32),
            dma((9,)),
            dma((3,)),
            dma((6 * CHUNKS + 2,)),
            dma((6 * CHUNKS + 2,)),
            dma,
            dma,
            dma,
            dma,
            dma((LAYERS,)),
            dma((LAYERS, 3)),
            dma((LAYERS, 3)),
            dma((LAYERS, 3)),
            dma((LAYERS,)),
            dma((LAYERS,)),
            pltpu.SemaphoreType.REGULAR((2, 2)),
        ],
        compiler_params=pltpu.CompilerParams(
            collective_id=0, has_side_effects=True, vmem_limit_bytes=60 * 1024 * 1024
        ),
    )(
        features,
        conv_weight.reshape(9, 3, D, D),
        queries,
        w_query,
        w_key,
        w_value,
        w_out,
        norm_gain.reshape(1, D),
        mask_weight,
        mask_blocks.T,
    )
    return embed, logits.reshape(NQ, 1, 2, NX)


def solution(mesh):
    return jax.shard_map(
        local,
        mesh=mesh,
        in_specs=(
            P("span", "qry", None, None),
            P(),
            P("qry", None),
            P(),
            P(),
            P(),
            P(),
            P(),
            P(),
            P(),
        ),
        out_specs=(P("qry", None), P(None, "span", "qry", None)),
        check_vma=False,
    )
```

```python
import jax
import jax.numpy as jnp
from jax import lax
from jax.experimental import pallas as pl
from jax.experimental.pallas import tpu as pltpu
from jax.sharding import PartitionSpec as P

MESH = pl.DeviceIdType.MESH
HEADS = 8
LAYERS = 2
D = 256
HEAD_DIM = 32
NX = 128
NQ = 128
MB = 4
NY = 32
SPAN = 16
QRY = 16
F32 = jnp.float32
BF16 = jnp.bfloat16
ZS = 8
CHUNKS = 4
Z_ORDER = (0, 1, 7, 2, 6, 3, 5, 4)
GROUPS = ((0, 8), (8, 14), (14, 16))
PLACE_GROUP = (0, 0, 0, 0, 1, 1, 1, 2)
Z_SENDS = (4, 3, 5, 2, 6, 1, 7)
XY_SENDS = sorted(
    ((dy, dx) for dy in range(4) for dx in range(4) if dy or dx),
    key=lambda t: -(min(t[0], 4 - t[0]) + min(t[1], 4 - t[1])),
)


def iota(shape, dim):
    return lax.broadcasted_iota(jnp.int32, shape, dim)


def dot(a, b):
    return jnp.dot(a, b, preferred_element_type=F32)


def dot_nt(a, b):
    return lax.dot_general(a, b, (((1,), (1,)), ((), ())), preferred_element_type=F32)


def wrap(i, n):
    return lax.rem(i + n, n)


def slot_plane(slot, z):
    place = slot // 2
    offset = jnp.zeros_like(slot)
    for k, dz in enumerate(Z_ORDER):
        offset = jnp.where(place == k, dz, offset)
    return ((z + offset) % ZS) * 2 + slot % 2


def merge(ids, near, mid, far, pair_id, term_y, lane_z):
    rows = ids.shape[0]
    flat = far.reshape(QRY * 16, 128)
    raised = pltpu.roll(flat.astype(F32), QRY * 16 - 4, axis=0).astype(BF16)
    outs = jnp.concatenate(
        [
            jnp.concatenate([near[half].reshape(QRY * 16, 128) for half in range(2)], axis=1),
            jnp.concatenate(
                [mid[:, half * 16 : half * 16 + 16, :].reshape(QRY * 16, 128) for half in range(2)],
                axis=1,
            ),
            jnp.concatenate([flat, raised], axis=1),
        ],
        axis=0,
    )
    pick, term = [], []
    for j in range(MB):
        idj = ids[:, j : j + 1]
        pick.append(jnp.where(pair_id == idj, 1.0, 0.0).astype(BF16))
        term.append(jnp.where(term_y == idj % NY, 1.0, 0.0).astype(BF16))
    lse = dot(jnp.concatenate(term, axis=0), flat)
    chosen = dot(jnp.concatenate(pick, axis=0), outs)
    lses = []
    for j in range(MB):
        lj = jnp.where(lane_z == ids[:, j : j + 1] // NY, lse[j * rows : (j + 1) * rows], 0.0)
        for shift in (8, 16, 32, 64):
            lj = lj + pltpu.roll(lj, shift, axis=1)
        lses.append(lj)
    top = jnp.maximum(jnp.maximum(lses[0], lses[1]), jnp.maximum(lses[2], lses[3]))
    weights = [jnp.exp(lj - top) for lj in lses]
    inv = 1.0 / (weights[0] + weights[1] + weights[2] + weights[3])
    attn = jnp.zeros((rows, D), F32)
    for j in range(MB):
        wj = weights[j] * inv
        attn = attn + jnp.concatenate([wj, wj], axis=1) * chosen[j * rows : (j + 1) * rows]
    return attn


def kernel(
    feat_hbm, conv_hbm, queries_hbm, wq_hbm, wk_hbm, wv_hbm, wo_hbm, gain_hbm, mw_hbm, mb_hbm,
    embed_ref, logit_ref,
    ext, taps, qbuf, qpbuf, wq, wk, wv, wo, mw, gain, mb, wvp, wop, pix, keys, vals,
    stage1, near, mid, far, state, acc,
    local_sem, conv_sem, halo_send, halo_recv, q_send, q_recv, p_send, p_recv,
    s_send, s_recv, y_send, y_recv, c_send, c_recv, entered,
):
    s = lax.axis_index("span")
    q = lax.axis_index("qry")
    z, core = s // 2, lax.rem(s, 2)
    y, x = q // 4, lax.rem(q, 4)
    up, down = wrap(s + 1, SPAN), wrap(s - 1, SPAN)
    right, left = wrap(q + 1, QRY), wrap(q - 1, QRY)
    z_peers = [(d, c) for d in Z_SENDS for c in range(2)] + [(0, 1)]
    z_index = [wrap(z + d, ZS) * 2 + (c if d else 1 - core) for d, c in z_peers]
    xy_index = [lax.rem(y + dy, 4) * 4 + lax.rem(x + dx, 4) for dy, dx in XY_SENDS]

    barrier = pltpu.get_barrier_semaphore()
    for d in (1, -1, 2, -2):
        pl.semaphore_signal(barrier, inc=1, device_id=(wrap(s + d, SPAN), q), device_id_type=MESH)
    for block in xy_index[::-1]:
        pl.semaphore_signal(barrier, inc=1, device_id=(s, block), device_id_type=MESH)

    own = pltpu.make_async_copy(feat_hbm.at[0], ext.at[1, pl.ds(1, 2)], local_sem.at[0])
    own.start()
    early, loads = [], []
    for k, (src, dst) in enumerate(
        (
            (mb_hbm, mb),
            (queries_hbm, qbuf.at[q]),
            (wq_hbm, wq),
            (wv_hbm, wv),
            (wo_hbm, wo),
            (wk_hbm, wk),
            (mw_hbm, mw),
            (gain_hbm, gain),
        )
    ):
        copy = pltpu.make_async_copy(src, dst, local_sem.at[1 + k])
        copy.start()
        (early if k < 3 else loads).append(copy)
    conv_loads = [
        pltpu.make_async_copy(conv_hbm.at[:, dx], taps.at[dx], conv_sem.at[dx]) for dx in range(3)
    ]
    for load in conv_loads:
        load.start()
    pl.semaphore_wait(barrier, 4 + len(xy_index))

    def tell(step):
        for k, d in enumerate((2 * step, -2 * step)):
            pl.semaphore_signal(
                entered.at[step - 1, k], inc=1, device_id=(wrap(s + d, SPAN), q), device_id_type=MESH
            )

    def hear(step):
        for k in range(2):
            pl.semaphore_wait(entered.at[step - 1, k], 1)

    sends = []

    def send(src, dst, k, peer):
        copy = pltpu.make_async_remote_copy(
            src_ref=src, dst_ref=dst, send_sem=halo_send.at[k], recv_sem=halo_recv.at[k],
            device_id=peer, device_id_type=MESH,
        )
        copy.start()
        sends.append(copy)
        return copy

    rows = feat_hbm.at[0]
    chunks = [pl.ds(k * (NX // CHUNKS), NX // CHUNKS) for k in range(CHUNKS)]
    across = []
    for k, chunk in enumerate(chunks):
        across.append(send(rows.at[1, chunk], ext.at[1, 0, chunk], 2 * k, (s, right)))
        across.append(send(rows.at[0, chunk], ext.at[1, 3, chunk], 2 * k + 1, (s, left)))
    from_down = send(rows, ext.at[0, pl.ds(1, 2)], 2 * CHUNKS, (up, q))
    from_up = send(rows, ext.at[2, pl.ds(1, 2)], 2 * CHUNKS + 1, (down, q))

    tell(1)

    def to_plane(buf, send_sem, recv_sem):
        for block in xy_index:
            pltpu.make_async_remote_copy(
                src_ref=buf.at[q], dst_ref=buf.at[q], send_sem=send_sem, recv_sem=recv_sem,
                device_id=(s, block), device_id_type=MESH,
            ).start()

    def wait_slots(buf, count, sem):
        some = buf.at[pl.ds(0, count)]
        pltpu.make_async_copy(some, some, sem).wait()

    for load in early:
        load.wait()
    qproj = (dot(qbuf[q].astype(BF16), wq[0]) * HEAD_DIM**-0.5).astype(BF16)
    qpbuf[q] = jnp.concatenate([qproj[:, 0:128], qproj[:, 128:256]], axis=0)
    to_plane(qpbuf, p_send, p_recv)

    perm = jnp.where(
        iota((D, D), 1) == (iota((D, D), 0) % HEAD_DIM) * HEADS + iota((D, D), 0) // HEAD_DIM, 1.0, 0.0
    ).astype(BF16)
    perm_t = jnp.where(
        iota((D, D), 0) == (iota((D, D), 1) % HEAD_DIM) * HEADS + iota((D, D), 1) // HEAD_DIM, 1.0, 0.0
    ).astype(BF16)
    for load in loads:
        load.wait()
    for layer in range(LAYERS):
        wvp[layer] = dot(wv[layer], perm).astype(BF16)
        wop[layer] = dot(perm_t, wo[layer]).astype(BF16)

    lists = mb[...]
    all_ids = lists.astype(F32).T.astype(jnp.int32)
    own_ids, picks, listed = [], [], []
    for r in range(2):
        block_id = s * NY + q * 2 + r
        listed.append(jnp.max(jnp.where(all_ids == block_id, 1, 0), axis=1, keepdims=True) > 0)
        picks.append(jnp.max(jnp.where(lists == block_id, 1.0, 0.0), axis=0, keepdims=True))
        own_ids.append(jnp.sum(jnp.where(listed[r], all_ids.astype(F32), 0.0), axis=0, keepdims=True))
    own_ids = jnp.concatenate(own_ids + [jnp.full((6, MB), -1.0, F32)], axis=0).astype(jnp.int32)
    picks = jnp.concatenate(picks + [jnp.zeros((6, NQ), F32)], axis=0).astype(BF16)

    col = iota((1, QRY * 48), 1)
    group, kind = col // 256, col % 16
    slot = jnp.where(group < 2, group * 8 + col % 8, 14 + col % 2)
    half = jnp.where(group < 2, kind // 8, kind // 2)
    limit = jnp.where(group == 0, 8, jnp.where(group == 1, 6, 4))
    pair_id = slot_plane(slot, z) * NY + ((col % 256) // 16) * 2 + half
    pair_id = jnp.where(jnp.where(group < 2, col % 8, kind) < limit, pair_id, -2)
    row = iota((1, QRY * 16), 1)
    kind = row % 16 - 8
    term_y = (row // 16) * 2 + jnp.where(kind < 3, 0, 1)
    term_y = jnp.where((kind >= 0) & (kind < 6), term_y, -2)
    lane_z = slot_plane(iota((1, 128), 1) // HEADS, z)

    relays = []
    for k, copy in enumerate(across):
        copy.wait_recv()
        chunk, row = chunks[k // 2], 3 * (k % 2)
        first = 2 * CHUNKS + 2 + 2 * k
        relays.append(send(ext.at[1, row, chunk], ext.at[0, row, chunk], first, (up, q)))
        relays.append(send(ext.at[1, row, chunk], ext.at[2, row, chunk], first + 1, (down, q)))
    hear(1)
    tell(2)
    own.wait()
    for load in conv_loads:
        load.wait()

    middle = [ext[1, row] for row in range(4)]
    middle[0] = jnp.where(q > 0, middle[0], jnp.zeros_like(middle[0]))
    middle[3] = jnp.where(q < QRY - 1, middle[3], jnp.zeros_like(middle[3]))
    slab = jnp.concatenate(
        [jnp.concatenate(middle[dy : dy + 2], axis=0) for dy in range(3)], axis=1
    )
    for dx in range(3):
        acc[dx] = dot(slab, taps[dx, 3:6].reshape(3 * D, D))
    for dz, copy, outside in ((0, from_down, s == 0), (2, from_up, s == SPAN - 1)):
        copy.wait_recv()

        @pl.when(outside)
        def _():
            ext[dz, 1:3] = jnp.zeros((2, NX, D), BF16)

        pair = jnp.concatenate([ext[dz, 1], ext[dz, 2]], axis=1)
        for dx in range(3):
            for r in range(2):
                weights = taps[dx, 3 * dz + 1 - r : 3 * dz + 3 - r].reshape(2 * D, D)
                acc[dx, r * NX : (r + 1) * NX] += dot(pair, weights)

    for copy in relays:
        copy.wait_recv()

    @pl.when((s == 0) | (q == 0))
    def _():
        ext[0, 0] = jnp.zeros((NX, D), BF16)

    @pl.when((s == 0) | (q == QRY - 1))
    def _():
        ext[0, 3] = jnp.zeros((NX, D), BF16)

    @pl.when((s == SPAN - 1) | (q == 0))
    def _():
        ext[2, 0] = jnp.zeros((NX, D), BF16)

    @pl.when((s == SPAN - 1) | (q == QRY - 1))
    def _():
        ext[2, 3] = jnp.zeros((NX, D), BF16)

    def column(dx):
        parts = []
        for r in range(2):
            corner = jnp.concatenate([ext[0, 3 * r], ext[2, 3 * r]], axis=1)
            weights = jnp.concatenate([taps[dx, 2 * r], taps[dx, 6 + 2 * r]], axis=0)
            parts.append(acc[dx, r * NX : (r + 1) * NX] + dot(corner, weights))
        return jnp.concatenate(parts, axis=0)

    x_at = iota((2 * NX, D), 0) % NX
    conv = jnp.where(x_at == 0, 0.0, pltpu.roll(column(0), 1, axis=0))
    conv = conv + column(1)
    conv = conv + jnp.where(x_at == NX - 1, 0.0, pltpu.roll(column(2), 2 * NX - 1, axis=0))
    pixel = jnp.maximum(conv, 0.0).astype(BF16)
    pix[...] = pixel
    keys[0] = dot(pixel, wk[0]).astype(BF16)
    vals[0] = dot(pixel, wvp[0]).astype(BF16)

    wait_slots(qpbuf, QRY - 1, p_recv)
    projected = jnp.concatenate(
        [qpbuf[:, half * 8 : half * 8 + 8, :].astype(F32).reshape(NQ, 128) for half in range(2)], axis=1
    )
    qproj = dot(picks, projected.astype(BF16))

    head_of = iota((HEADS, D), 1) // HEAD_DIM == iota((HEADS, D), 0)
    head_of_lane = iota((HEADS, D), 1) % HEADS == iota((HEADS, D), 0)
    lse_lane = iota((HEADS, 128), 1) % HEADS == iota((HEADS, 128), 0)
    hear(2)
    for layer in range(LAYERS):
        spread = jnp.concatenate(
            [jnp.where(head_of, qproj[r : r + 1], 0.0) for r in range(2)], axis=0
        ).astype(BF16)
        scores = dot_nt(spread, keys[layer])
        scores = jnp.concatenate([scores[0:8, 0:NX], scores[8:16, NX : 2 * NX]], axis=0)
        top = jnp.max(scores, axis=1, keepdims=True)
        prob = jnp.exp(scores - top)
        total = jnp.sum(prob, axis=1, keepdims=True)
        inv = 1.0 / total
        lse = top + jnp.log(total)
        prob = prob.astype(BF16)
        low, high, lines = [], [], []
        for r in range(2):
            part = slice(r * HEADS, (r + 1) * HEADS)
            weighted = dot(prob[part], vals[layer, r * NX : (r + 1) * NX])
            out = jnp.sum(jnp.where(head_of_lane, weighted * inv[part], 0.0), axis=0, keepdims=True)
            low.append(out[:, 0:128])
            high.append(out[:, 128:256])
            lines.append(jnp.sum(jnp.where(lse_lane, lse[part], 0.0), axis=0, keepdims=True))
        buf = stage1.at[layer]
        buf[core] = jnp.concatenate(low + high + lines + [jnp.zeros((2, 128), F32)], axis=0)
        for (d, c), plane in zip(z_peers, z_index):
            place = Z_ORDER.index((ZS - d) % ZS)
            pltpu.make_async_remote_copy(
                src_ref=buf.at[core], dst_ref=buf.at[place * 2 + core],
                send_sem=s_send.at[layer], recv_sem=s_recv.at[layer, PLACE_GROUP[place]],
                device_id=(plane, q), device_id_type=MESH,
            ).start()
        if layer == 0:
            to_plane(qbuf, q_send, q_recv)
            keys[1] = dot(pix[...], wk[1]).astype(BF16)
            vals[1] = dot(pix[...], wvp[1]).astype(BF16)
        else:
            attn = merge(all_ids, near[0], mid[0], far[0], pair_id, term_y, lane_z)
            state[...] = qbuf[...].reshape(NQ, D) + dot(attn.astype(BF16), wop[0])
        lines = [jnp.zeros((1, 128), F32)] * 2
        for group, (start, end) in enumerate(GROUPS):
            count = end - start
            wait_slots(buf, count - (group == 0), s_recv.at[layer, group])
            got = stage1[layer, start:end]
            parts = [got[:, k, :] for k in range(4)]
            own_lanes = iota((count, 128), 1) // HEADS == start + iota((count, 128), 0)
            for r in range(2):
                kept = jnp.where(own_lanes, got[:, 4 + r, :], 0.0)
                lines[r] = lines[r] + jnp.sum(kept, axis=0, keepdims=True)
            if group == 0:
                halves = [jnp.concatenate(parts[2 * k : 2 * k + 2], axis=0) for k in range(2)]
                near[layer, core, q] = jnp.where(core == 0, halves[0], halves[1]).astype(BF16)
                to_plane(near.at[layer, core], y_send.at[layer, 0], y_recv.at[layer, 0])
            elif group == 1:
                blank = jnp.zeros((2, 128), F32)
                message = [piece for part in parts for piece in (part, blank)]
                mid[layer, q] = jnp.concatenate(message, axis=0).astype(BF16)
                to_plane(mid.at[layer], y_send.at[layer, 1], y_recv.at[layer, 1])
        message = parts
        for line in lines:
            for _ in range(3):
                term = line.astype(BF16).astype(F32)
                message.append(term)
                line = line - term
        message.append(jnp.zeros((2, 128), F32))
        far[layer, q] = jnp.concatenate(message, axis=0).astype(BF16)
        to_plane(far.at[layer], y_send.at[layer, 2], y_recv.at[layer, 2])
        if layer == 0:
            wait_slots(qbuf, QRY - 1, q_recv)
            state_all = qbuf[...].reshape(NQ, D)
            own_state = [
                jnp.sum(jnp.where(listed[r], state_all, 0.0), axis=0, keepdims=True) for r in range(2)
            ]
            own_state = jnp.concatenate(own_state + [jnp.zeros((6, D), F32)], axis=0)
        wait_slots(near.at[layer, 0], QRY - 1, y_recv.at[layer, 0])
        swap = pltpu.make_async_remote_copy(
            src_ref=near.at[layer, core], dst_ref=near.at[layer, core],
            send_sem=c_send.at[layer], recv_sem=c_recv.at[layer],
            device_id=(z * 2 + 1 - core, q), device_id_type=MESH,
        )
        swap.start()
        sends.append(swap)
        wait_slots(mid.at[layer], QRY - 1, y_recv.at[layer, 1])
        wait_slots(far.at[layer], QRY - 1, y_recv.at[layer, 2])
        swap.wait_recv()
        if layer == 0:
            attn = merge(own_ids, near[0], mid[0], far[0], pair_id, term_y, lane_z)
            own_state = own_state + dot(attn.astype(BF16), wop[0])
            qproj = (dot(own_state.astype(BF16), wq[1]) * HEAD_DIM**-0.5).astype(BF16).astype(F32)

    attn = merge(all_ids, near[1], mid[1], far[1], pair_id, term_y, lane_z)
    final = state[...] + dot(attn.astype(BF16), wop[1])
    mean = jnp.mean(final, axis=-1, keepdims=True)
    centered = final - mean
    var = jnp.mean(centered * centered, axis=-1, keepdims=True)
    embed = centered * lax.rsqrt(var + 1e-05) * gain[...]
    state[...] = embed
    embed_ref[...] = state[pl.ds(pl.multiple_of(q * 8, 8), 8), :]
    mask_embed = dot(embed.astype(BF16), mw[...]).astype(BF16)
    logit_ref[...] = (dot_nt(mask_embed, pix[...]) * D**-0.5).astype(BF16)

    for copy in sends:
        copy.wait_send()
    wait_slots(qbuf, QRY - 1, q_send)
    wait_slots(qpbuf, QRY - 1, p_send)
    for layer in range(LAYERS):
        wait_slots(stage1.at[layer], SPAN - 1, s_send.at[layer])
        wait_slots(near.at[layer, 0], QRY - 1, y_send.at[layer, 0])
        wait_slots(mid.at[layer], QRY - 1, y_send.at[layer, 1])
        wait_slots(far.at[layer], QRY - 1, y_send.at[layer, 2])


def local(
    features, conv_weight, queries, w_query, w_key, w_value, w_out, norm_gain, mask_weight, mask_blocks
):
    hbm = pl.BlockSpec(memory_space=pltpu.HBM)
    vmem = pl.BlockSpec(memory_space=pltpu.VMEM)
    dma = pltpu.SemaphoreType.DMA
    square = pltpu.VMEM((LAYERS, D, D), BF16)
    embed, logits = pl.pallas_call(
        kernel,
        out_shape=(
            jax.ShapeDtypeStruct((8, D), F32),
            jax.ShapeDtypeStruct((NQ, 2 * NX), BF16),
        ),
        in_specs=[hbm] * 10,
        out_specs=(vmem, vmem),
        scratch_shapes=[
            pltpu.VMEM((3, 4, NX, D), BF16),
            pltpu.VMEM((3, 9, D, D), BF16),
            pltpu.VMEM((QRY, 8, D), F32),
            pltpu.VMEM((QRY, 16, 128), BF16),
            square,
            square,
            square,
            square,
            pltpu.VMEM((D, D), BF16),
            pltpu.VMEM((1, D), F32),
            pltpu.VMEM((MB, NQ), jnp.int32),
            square,
            square,
            pltpu.VMEM((2 * NX, D), BF16),
            square,
            square,
            pltpu.VMEM((LAYERS, SPAN, 8, 128), F32),
            pltpu.VMEM((LAYERS, 2, QRY, 16, 128), BF16),
            pltpu.VMEM((LAYERS, QRY, 32, 128), BF16),
            pltpu.VMEM((LAYERS, QRY, 16, 128), BF16),
            pltpu.VMEM((NQ, D), F32),
            pltpu.VMEM((3, 2 * NX, D), F32),
            dma((9,)),
            dma((3,)),
            dma((6 * CHUNKS + 2,)),
            dma((6 * CHUNKS + 2,)),
            dma,
            dma,
            dma,
            dma,
            dma((LAYERS,)),
            dma((LAYERS, 3)),
            dma((LAYERS, 3)),
            dma((LAYERS, 3)),
            dma((LAYERS,)),
            dma((LAYERS,)),
            pltpu.SemaphoreType.REGULAR((2, 2)),
        ],
        compiler_params=pltpu.CompilerParams(
            collective_id=0, has_side_effects=True, vmem_limit_bytes=40 * 1024 * 1024
        ),
    )(
        *(
            pltpu.with_memory_space_constraint(operand, pltpu.HBM)
            for operand in (
                features,
                conv_weight.reshape(9, 3, D, D),
                queries,
                w_query,
                w_key,
                w_value,
                w_out,
                norm_gain.reshape(1, D),
                mask_weight,
                mask_blocks.T,
            )
        )
    )
    return embed, logits.reshape(NQ, 1, 2, NX)


def solution(mesh):
    return jax.shard_map(
        local,
        mesh=mesh,
        in_specs=(
            P("span", "qry", None, None),
            P(),
            P("qry", None),
            P(),
            P(),
            P(),
            P(),
            P(),
            P(),
            P(),
        ),
        out_specs=(P("qry", None), P(None, "span", "qry", None)),
        check_vma=False,
    )
```

```python
import jax
import jax.numpy as jnp
from jax import lax
from jax.experimental import pallas as pl
from jax.experimental.pallas import tpu as pltpu
from jax.sharding import PartitionSpec as P

MESH = pl.DeviceIdType.MESH
HEADS = 8
LAYERS = 2
D = 256
HEAD_DIM = 32
NX = 128
NQ = 128
MB = 4
NY = 32
SPAN = 16
QRY = 16
F32 = jnp.float32
BF16 = jnp.bfloat16
ZS = 8
CHUNKS = 4
Z_ORDER = (0, 1, 7, 2, 6, 3, 5, 4)
GROUPS = ((0, 6), (6, 10), (10, 14), (14, 16))
PLACE_GROUP = (0, 0, 0, 1, 1, 2, 2, 3)
Z_SENDS = (4, 3, 5, 2, 6, 1, 7)
XY_SENDS = sorted(
    ((dy, dx) for dy in range(4) for dx in range(4) if dy or dx),
    key=lambda t: -(min(t[0], 4 - t[0]) + min(t[1], 4 - t[1])),
)


def iota(shape, dim):
    return lax.broadcasted_iota(jnp.int32, shape, dim)


def dot(a, b):
    return jnp.dot(a, b, preferred_element_type=F32)


def dot_nt(a, b):
    return lax.dot_general(a, b, (((1,), (1,)), ((), ())), preferred_element_type=F32)


def wrap(i, n):
    return lax.rem(i + n, n)


def slot_plane(slot, z):
    place = slot // 2
    offset = jnp.zeros_like(slot)
    for k, dz in enumerate(Z_ORDER):
        offset = jnp.where(place == k, dz, offset)
    return ((z + offset) % ZS) * 2 + slot % 2


def choices(ids, pair_id, term_y):
    pick, term = [], []
    for j in range(MB):
        idj = ids[:, j : j + 1]
        pick.append(jnp.where(pair_id == idj, 1.0, 0.0).astype(BF16))
        term.append(jnp.where(term_y == idj % NY, 1.0, 0.0).astype(BF16))
    return jnp.concatenate(pick, axis=0), jnp.concatenate(term, axis=0)


def both_halves(block, rows):
    flat = block.reshape(QRY * 16, 128)
    raised = pltpu.roll(flat.astype(F32), QRY * 16 - rows, axis=0).astype(BF16)
    return jnp.concatenate([flat, raised], axis=1)


def choose_early(pick, near, mid):
    outs = jnp.concatenate(
        [
            both_halves(mid[0], 8),
            both_halves(mid[1], 8),
            jnp.concatenate([near[half].reshape(QRY * 16, 128) for half in range(2)], axis=1),
        ],
        axis=0,
    )
    return dot(pick, outs)


def merge(ids, chosen, pick, term, far, lane_z):
    rows = ids.shape[0]
    lse = dot(term, far.reshape(QRY * 16, 128))
    chosen = chosen + dot(pick, both_halves(far, 4))
    lses = []
    for j in range(MB):
        lj = jnp.where(lane_z == ids[:, j : j + 1] // NY, lse[j * rows : (j + 1) * rows], 0.0)
        for shift in (8, 16, 32, 64):
            lj = lj + pltpu.roll(lj, shift, axis=1)
        lses.append(lj)
    top = jnp.maximum(jnp.maximum(lses[0], lses[1]), jnp.maximum(lses[2], lses[3]))
    weights = [jnp.exp(lj - top) for lj in lses]
    inv = 1.0 / (weights[0] + weights[1] + weights[2] + weights[3])
    attn = jnp.zeros((rows, D), F32)
    for j in range(MB):
        wj = weights[j] * inv
        attn = attn + jnp.concatenate([wj, wj], axis=1) * chosen[j * rows : (j + 1) * rows]
    return attn


def kernel(
    feat_hbm, conv_hbm, queries_hbm, wq_hbm, wk_hbm, wv_hbm, wo_hbm, gain_hbm, mw_hbm, mb_hbm,
    embed_ref, logit_ref,
    ext, taps, qbuf, qpbuf, wq, wk, wv, wo, mw, gain, mb, wvp, wop, pix, pix_t, keys, vals,
    stage1, near, mid, far, state, acc, pick_all, term_all, woven,
    local_sem, conv_sem, halo_send, halo_recv, q_send, q_recv, p_send, p_recv,
    s_send, s_recv, y_send, y_recv, c_send, c_recv, entered,
):
    s = lax.axis_index("span")
    q = lax.axis_index("qry")
    z, core = s // 2, lax.rem(s, 2)
    y, x = q // 4, lax.rem(q, 4)
    up, down = wrap(s + 1, SPAN), wrap(s - 1, SPAN)
    right, left = wrap(q + 1, QRY), wrap(q - 1, QRY)
    z_peers = [(d, c) for d in Z_SENDS for c in range(2)] + [(0, 1)]
    z_index = [wrap(z + d, ZS) * 2 + (c if d else 1 - core) for d, c in z_peers]
    xy_index = [lax.rem(y + dy, 4) * 4 + lax.rem(x + dx, 4) for dy, dx in XY_SENDS]

    barrier = pltpu.get_barrier_semaphore()
    for d in (1, -1, 2, -2, 3, -3, 4, -4):
        pl.semaphore_signal(barrier, inc=1, device_id=(wrap(s + d, SPAN), q), device_id_type=MESH)
    for block in xy_index[::-1]:
        pl.semaphore_signal(barrier, inc=1, device_id=(s, block), device_id_type=MESH)

    own = pltpu.make_async_copy(feat_hbm.at[0], ext.at[1, pl.ds(1, 2)], local_sem.at[0])
    own.start()
    first_loads, loads = [], []
    for k, (src, dst) in enumerate(
        (
            (mb_hbm, mb),
            (queries_hbm, qbuf.at[q]),
            (wq_hbm, wq),
            (wv_hbm, wv),
            (wo_hbm, wo),
            (wk_hbm, wk),
            (mw_hbm, mw),
            (gain_hbm, gain),
        )
    ):
        copy = pltpu.make_async_copy(src, dst, local_sem.at[1 + k])
        copy.start()
        (first_loads if k < 3 else loads).append(copy)
    conv_loads = [
        pltpu.make_async_copy(conv_hbm.at[:, dx], taps.at[dx], conv_sem.at[dx]) for dx in range(3)
    ]
    for load in conv_loads:
        load.start()
    pl.semaphore_wait(barrier, 8 + len(xy_index))

    for k, d in enumerate((4, -4)):
        pl.semaphore_signal(entered.at[k], inc=1, device_id=(wrap(s + d, SPAN), q), device_id_type=MESH)

    sends = []

    def send(src, dst, k, peer):
        copy = pltpu.make_async_remote_copy(
            src_ref=src, dst_ref=dst, send_sem=halo_send.at[k], recv_sem=halo_recv.at[k],
            device_id=peer, device_id_type=MESH,
        )
        copy.start()
        sends.append(copy)
        return copy

    rows = feat_hbm.at[0]
    chunks = [pl.ds(k * (NX // CHUNKS), NX // CHUNKS) for k in range(CHUNKS)]
    across = []
    for k, chunk in enumerate(chunks):
        across.append(send(rows.at[1, chunk], ext.at[1, 0, chunk], 2 * k, (s, right)))
        across.append(send(rows.at[0, chunk], ext.at[1, 3, chunk], 2 * k + 1, (s, left)))
    from_down = send(rows, ext.at[0, pl.ds(1, 2)], 2 * CHUNKS, (up, q))
    from_up = send(rows, ext.at[2, pl.ds(1, 2)], 2 * CHUNKS + 1, (down, q))

    def to_plane(buf, send_sem, recv_sem):
        for block in xy_index:
            pltpu.make_async_remote_copy(
                src_ref=buf.at[q], dst_ref=buf.at[q], send_sem=send_sem, recv_sem=recv_sem,
                device_id=(s, block), device_id_type=MESH,
            ).start()

    def wait_slots(buf, count, sem):
        some = buf.at[pl.ds(0, count)]
        pltpu.make_async_copy(some, some, sem).wait()

    for load in first_loads:
        load.wait()
    qproj = (dot(qbuf[q].astype(BF16), wq[0]) * HEAD_DIM**-0.5).astype(BF16)
    qpbuf[q] = jnp.concatenate([qproj[:, 0:128], qproj[:, 128:256]], axis=0)
    to_plane(qpbuf, p_send, p_recv)

    perm = jnp.where(
        iota((D, D), 1) == (iota((D, D), 0) % HEAD_DIM) * HEADS + iota((D, D), 0) // HEAD_DIM, 1.0, 0.0
    ).astype(BF16)
    perm_t = jnp.where(
        iota((D, D), 0) == (iota((D, D), 1) % HEAD_DIM) * HEADS + iota((D, D), 1) // HEAD_DIM, 1.0, 0.0
    ).astype(BF16)
    for load in loads:
        load.wait()
    for layer in range(LAYERS):
        wvp[layer] = dot(wv[layer], perm).astype(BF16)
        wop[layer] = dot(perm_t, wo[layer]).astype(BF16)

    lists = mb[...]
    all_ids = lists.astype(F32).T.astype(jnp.int32)
    own_ids, picks, listed = [], [], []
    for r in range(2):
        block_id = s * NY + q * 2 + r
        listed.append(jnp.max(jnp.where(all_ids == block_id, 1, 0), axis=1, keepdims=True) > 0)
        picks.append(jnp.max(jnp.where(lists == block_id, 1.0, 0.0), axis=0, keepdims=True))
        own_ids.append(jnp.sum(jnp.where(listed[r], all_ids.astype(F32), 0.0), axis=0, keepdims=True))
    own_ids = jnp.concatenate(own_ids + [jnp.full((6, MB), -1.0, F32)], axis=0).astype(jnp.int32)
    picks = jnp.concatenate(picks + [jnp.zeros((6, NQ), F32)], axis=0).astype(BF16)

    col = iota((1, QRY * 64), 1)
    group, kind = col // 256, col % 16
    group = jnp.where(group == 3, 3, jnp.where(group == 2, 0, group + 1))
    width = jnp.where(group == 0, 8, jnp.where(group == 3, 2, 4))
    place = kind & (width - 1)
    half = (kind - place) // width
    pair_id = slot_plane(jnp.where(group == 0, 0, 2 + 4 * group) + place, z) * NY + ((col % 256) // 16) * 2 + half
    valid = jnp.where(half < 2, place, 8) < jnp.where(group == 0, 6, width)
    pair_id = jnp.where(valid, pair_id, -2)
    row = iota((1, QRY * 16), 1)
    kind = row % 16 - 8
    term_y = (row // 16) * 2 + jnp.where(kind < 3, 0, 1)
    term_y = jnp.where((kind >= 0) & (kind < 6), term_y, -2)
    lane_z = slot_plane(iota((1, 128), 1) // HEADS, z)
    own_pick, own_term = choices(own_ids, pair_id, term_y)

    relays = []
    for k, copy in enumerate(across):
        copy.wait_recv()
        chunk, row = chunks[k // 2], 3 * (k % 2)
        first = 2 * CHUNKS + 2 + 2 * k
        relays.append(send(ext.at[1, row, chunk], ext.at[0, row, chunk], first, (up, q)))
        relays.append(send(ext.at[1, row, chunk], ext.at[2, row, chunk], first + 1, (down, q)))
    own.wait()
    for load in conv_loads:
        load.wait()

    middle = [ext[1, row] for row in range(4)]
    middle[0] = jnp.where(q > 0, middle[0], jnp.zeros_like(middle[0]))
    middle[3] = jnp.where(q < QRY - 1, middle[3], jnp.zeros_like(middle[3]))
    slab = jnp.concatenate(
        [jnp.concatenate(middle[dy : dy + 2], axis=0) for dy in range(3)], axis=1
    )
    for dx in range(3):
        acc[dx] = dot(slab, taps[dx, 3:6].reshape(3 * D, D))
    for dz, copy, outside in ((0, from_down, s == 0), (2, from_up, s == SPAN - 1)):
        copy.wait_recv()

        @pl.when(outside)
        def _():
            ext[dz, 1:3] = jnp.zeros((2, NX, D), BF16)

        pair = jnp.concatenate([ext[dz, 1], ext[dz, 2]], axis=1)
        for dx in range(3):
            for r in range(2):
                weights = taps[dx, 3 * dz + 1 - r : 3 * dz + 3 - r].reshape(2 * D, D)
                acc[dx, r * NX : (r + 1) * NX] += dot(pair, weights)

    for copy in relays:
        copy.wait_recv()

    @pl.when((s == 0) | (q == 0))
    def _():
        ext[0, 0] = jnp.zeros((NX, D), BF16)

    @pl.when((s == 0) | (q == QRY - 1))
    def _():
        ext[0, 3] = jnp.zeros((NX, D), BF16)

    @pl.when((s == SPAN - 1) | (q == 0))
    def _():
        ext[2, 0] = jnp.zeros((NX, D), BF16)

    @pl.when((s == SPAN - 1) | (q == QRY - 1))
    def _():
        ext[2, 3] = jnp.zeros((NX, D), BF16)

    def column(dx):
        parts = []
        for r in range(2):
            corner = jnp.concatenate([ext[0, 3 * r], ext[2, 3 * r]], axis=1)
            weights = jnp.concatenate([taps[dx, 2 * r], taps[dx, 6 + 2 * r]], axis=0)
            parts.append(acc[dx, r * NX : (r + 1) * NX] + dot(corner, weights))
        return jnp.concatenate(parts, axis=0)

    x_at = iota((2 * NX, D), 0) % NX
    conv = jnp.where(x_at == 0, 0.0, pltpu.roll(column(0), 1, axis=0))
    conv = conv + column(1)
    conv = conv + jnp.where(x_at == NX - 1, 0.0, pltpu.roll(column(2), 2 * NX - 1, axis=0))
    pixel = jnp.maximum(conv, 0.0).astype(BF16)
    pix[...] = pixel
    keys[0] = dot(pixel, wk[0]).astype(BF16)
    vals[0] = dot(pixel, wvp[0]).astype(BF16)

    wait_slots(qpbuf, QRY - 1, p_recv)
    projected = jnp.concatenate(
        [qpbuf[:, half * 8 : half * 8 + 8, :].astype(F32).reshape(NQ, 128) for half in range(2)], axis=1
    )
    qproj = dot(picks, projected.astype(BF16))

    head_of = iota((HEADS, D), 1) // HEAD_DIM == iota((HEADS, D), 0)
    head_of_lane = iota((HEADS, D), 1) % HEADS == iota((HEADS, D), 0)
    lse_lane = iota((HEADS, 128), 1) % HEADS == iota((HEADS, 128), 0)
    for k in range(2):
        pl.semaphore_wait(entered.at[k], 1)
    for layer in range(LAYERS):
        spread = jnp.concatenate(
            [jnp.where(head_of, qproj[r : r + 1], 0.0) for r in range(2)], axis=0
        ).astype(BF16)
        scores = dot_nt(spread, keys[0]) if layer == 0 else dot(spread, keys[1])
        scores = jnp.concatenate([scores[0:8, 0:NX], scores[8:16, NX : 2 * NX]], axis=0)
        top = jnp.max(scores, axis=1, keepdims=True)
        prob = jnp.exp(scores - top)
        total = jnp.sum(prob, axis=1, keepdims=True)
        inv = 1.0 / total
        lse = top + jnp.log(total)
        prob = prob.astype(BF16)
        low, high, lines = [], [], []
        for r in range(2):
            part = slice(r * HEADS, (r + 1) * HEADS)
            weighted = dot(prob[part], vals[layer, r * NX : (r + 1) * NX])
            out = jnp.sum(jnp.where(head_of_lane, weighted * inv[part], 0.0), axis=0, keepdims=True)
            low.append(out[:, 0:128])
            high.append(out[:, 128:256])
            lines.append(jnp.sum(jnp.where(lse_lane, lse[part], 0.0), axis=0, keepdims=True))
        buf = stage1.at[layer]
        buf[core] = jnp.concatenate(low + high + lines + [jnp.zeros((2, 128), F32)], axis=0)
        for (d, c), plane in zip(z_peers, z_index):
            place = Z_ORDER.index((ZS - d) % ZS)
            pltpu.make_async_remote_copy(
                src_ref=buf.at[core], dst_ref=buf.at[place * 2 + core],
                send_sem=s_send.at[layer], recv_sem=s_recv.at[layer, PLACE_GROUP[place]],
                device_id=(plane, q), device_id_type=MESH,
            ).start()
        if layer == 0:
            to_plane(qbuf, q_send, q_recv)
            keys[1] = dot(pix[...], wk[1]).T.astype(BF16)
            pix_t[...] = pix[...].astype(F32).T.astype(BF16)
            vals[1] = dot(pix[...], wvp[1]).astype(BF16)
            pick_all[...], term_all[...] = choices(all_ids, pair_id, term_y)
        else:
            chosen = choose_early(pick_all[:, : QRY * 48], near[0], mid[0])
            attn = merge(all_ids, chosen, pick_all[:, QRY * 48 :], term_all[...], far[0], lane_z)
            state[...] = qbuf[...].reshape(NQ, D) + dot(attn.astype(BF16), wop[0])
        lines = [jnp.zeros((1, 128), F32)] * 2
        for group, (start, end) in enumerate(GROUPS):
            count = end - start
            wait_slots(buf, count - (group == 0), s_recv.at[layer, group])
            got = stage1[layer, start:end]
            parts = [got[:, k, :] for k in range(4)]
            own_lanes = iota((count, 128), 1) // HEADS == start + iota((count, 128), 0)
            for r in range(2):
                kept = jnp.where(own_lanes, got[:, 4 + r, :], 0.0)
                lines[r] = lines[r] + jnp.sum(kept, axis=0, keepdims=True)
            if group == 0:
                blank = jnp.zeros((2, 128), F32)
                halves = [
                    jnp.concatenate([parts[2 * k], blank, parts[2 * k + 1], blank], axis=0) for k in range(2)
                ]
                near[layer, core, q] = jnp.where(core == 0, halves[0], halves[1]).astype(BF16)
                to_plane(near.at[layer, core], y_send.at[layer, 0], y_recv.at[layer, 0])
            elif group < 3:
                mid[layer, group - 1, q] = jnp.concatenate(parts, axis=0).astype(BF16)
                to_plane(mid.at[layer, group - 1], y_send.at[layer, group], y_recv.at[layer, group])
        message = parts
        for line in lines:
            for _ in range(3):
                term = line.astype(BF16).astype(F32)
                message.append(term)
                line = line - term
        message.append(jnp.zeros((2, 128), F32))
        far[layer, q] = jnp.concatenate(message, axis=0).astype(BF16)
        to_plane(far.at[layer], y_send.at[layer, 3], y_recv.at[layer, 3])
        if layer == 0:
            wait_slots(qbuf, QRY - 1, q_recv)
            state_all = qbuf[...].reshape(NQ, D)
            own_state = [
                jnp.sum(jnp.where(listed[r], state_all, 0.0), axis=0, keepdims=True) for r in range(2)
            ]
            own_state = jnp.concatenate(own_state + [jnp.zeros((6, D), F32)], axis=0)
        wait_slots(near.at[layer, 0], QRY - 1, y_recv.at[layer, 0])
        swap = pltpu.make_async_remote_copy(
            src_ref=near.at[layer, core], dst_ref=near.at[layer, core],
            send_sem=c_send.at[layer], recv_sem=c_recv.at[layer],
            device_id=(z * 2 + 1 - core, q), device_id_type=MESH,
        )
        swap.start()
        sends.append(swap)
        for k in range(2):
            wait_slots(mid.at[layer, k], QRY - 1, y_recv.at[layer, 1 + k])
        swap.wait_recv()
        early = own_pick[:, : QRY * 48] if layer == 0 else pick_all[:, : QRY * 48]
        chosen = choose_early(early, near[layer], mid[layer])
        wait_slots(far.at[layer], QRY - 1, y_recv.at[layer, 3])
        if layer == 0:
            attn = merge(own_ids, chosen, own_pick[:, QRY * 48 :], own_term, far[0], lane_z)
            own_state = own_state + dot(attn.astype(BF16), wop[0])
            qproj = (dot(own_state.astype(BF16), wq[1]) * HEAD_DIM**-0.5).astype(BF16).astype(F32)

    attn = merge(all_ids, chosen, pick_all[:, QRY * 48 :], term_all[...], far[1], lane_z)
    final = state[...] + dot(attn.astype(BF16), wop[1])
    mean = jnp.mean(final, axis=-1, keepdims=True)
    centered = final - mean
    var = jnp.mean(centered * centered, axis=-1, keepdims=True)
    embed = centered * lax.rsqrt(var + 1e-05) * gain[...]
    state[...] = embed
    embed_ref[...] = state[pl.ds(pl.multiple_of(q * 8, 8), 8), :]
    mask_embed = dot(embed.astype(BF16), mw[...]).astype(BF16)
    logits = dot(mask_embed, pix_t[...]) * D**-0.5
    for r in range(2):
        woven[pl.ds(r, NQ, stride=2), :] = logits[:, r * NX : (r + 1) * NX]
    logit_ref[...] = woven[...].astype(BF16)

    for copy in sends:
        copy.wait_send()
    wait_slots(qbuf, QRY - 1, q_send)
    wait_slots(qpbuf, QRY - 1, p_send)
    for layer in range(LAYERS):
        wait_slots(stage1.at[layer], SPAN - 1, s_send.at[layer])
        wait_slots(near.at[layer, 0], QRY - 1, y_send.at[layer, 0])
        for k in range(2):
            wait_slots(mid.at[layer, k], QRY - 1, y_send.at[layer, 1 + k])
        wait_slots(far.at[layer], QRY - 1, y_send.at[layer, 3])


def hand_over(embed_ref, logit_ref, embed_out, logit_out, sem):
    copies = [
        pltpu.make_async_copy(logit_ref, logit_out, sem.at[0]),
        pltpu.make_async_copy(embed_ref, embed_out, sem.at[1]),
    ]
    for copy in copies:
        copy.start()
    for copy in copies:
        copy.wait()


def local(
    features, conv_weight, queries, w_query, w_key, w_value, w_out, norm_gain, mask_weight, mask_blocks
):
    hbm = pl.BlockSpec(memory_space=pltpu.HBM)
    vmem = pl.BlockSpec(memory_space=pltpu.VMEM)
    dma = pltpu.SemaphoreType.DMA
    square = pltpu.VMEM((LAYERS, D, D), BF16)
    embed, logits = pl.pallas_call(
        kernel,
        out_shape=(
            jax.ShapeDtypeStruct((8, D), F32),
            jax.ShapeDtypeStruct((2 * NQ, NX), BF16),
        ),
        in_specs=[hbm] * 10,
        out_specs=(vmem, vmem),
        scratch_shapes=[
            pltpu.VMEM((3, 4, NX, D), BF16),
            pltpu.VMEM((3, 9, D, D), BF16),
            pltpu.VMEM((QRY, 8, D), F32),
            pltpu.VMEM((QRY, 16, 128), BF16),
            square,
            square,
            square,
            square,
            pltpu.VMEM((D, D), BF16),
            pltpu.VMEM((1, D), F32),
            pltpu.VMEM((MB, NQ), jnp.int32),
            square,
            square,
            pltpu.VMEM((2 * NX, D), BF16),
            pltpu.VMEM((D, 2 * NX), BF16),
            square,
            square,
            pltpu.VMEM((LAYERS, SPAN, 8, 128), F32),
            pltpu.VMEM((LAYERS, 2, QRY, 16, 128), BF16),
            pltpu.VMEM((LAYERS, 2, QRY, 16, 128), BF16),
            pltpu.VMEM((LAYERS, QRY, 16, 128), BF16),
            pltpu.VMEM((NQ, D), F32),
            pltpu.VMEM((3, 2 * NX, D), F32),
            pltpu.VMEM((MB * NQ, QRY * 64), BF16),
            pltpu.VMEM((MB * NQ, QRY * 16), BF16),
            pltpu.VMEM((2 * NQ, NX), F32),
            dma((9,)),
            dma((3,)),
            dma((6 * CHUNKS + 2,)),
            dma((6 * CHUNKS + 2,)),
            dma,
            dma,
            dma,
            dma,
            dma((LAYERS,)),
            dma((LAYERS, 4)),
            dma((LAYERS, 4)),
            dma((LAYERS, 4)),
            dma((LAYERS,)),
            dma((LAYERS,)),
            pltpu.SemaphoreType.REGULAR((2,)),
        ],
        compiler_params=pltpu.CompilerParams(
            collective_id=0, has_side_effects=True, vmem_limit_bytes=40 * 1024 * 1024
        ),
    )(
        *(
            pltpu.with_memory_space_constraint(operand, pltpu.HBM)
            for operand in (
                features,
                conv_weight.reshape(9, 3, D, D),
                queries,
                w_query,
                w_key,
                w_value,
                w_out,
                norm_gain.reshape(1, D),
                mask_weight,
                mask_blocks.T,
            )
        )
    )
    embed, logits = pl.pallas_call(
        hand_over,
        out_shape=(
            jax.ShapeDtypeStruct((8, D), F32),
            jax.ShapeDtypeStruct((2 * NQ, NX), BF16),
        ),
        in_specs=[vmem] * 2,
        out_specs=(pl.BlockSpec(memory_space=pl.ANY),) * 2,
        scratch_shapes=[dma((2,))],
    )(*(pltpu.with_memory_space_constraint(part, pltpu.VMEM) for part in (embed, logits)))
    return embed, logits.reshape(NQ, 1, 2, NX)


def solution(mesh):
    return jax.shard_map(
        local,
        mesh=mesh,
        in_specs=(
            P("span", "qry", None, None),
            P(),
            P("qry", None),
            P(),
            P(),
            P(),
            P(),
            P(),
            P(),
            P(),
        ),
        out_specs=(P("qry", None), P(None, "span", "qry", None)),
        check_vma=False,
    )
```

```python
import jax
import jax.numpy as jnp
from jax import lax
from jax.experimental import pallas as pl
from jax.experimental.pallas import tpu as pltpu
from jax.sharding import PartitionSpec as P

MESH = pl.DeviceIdType.MESH
HEADS = 8
LAYERS = 2
D = 256
HEAD_DIM = 32
NX = 128
NQ = 128
MB = 4
NY = 32
SPAN = 16
QRY = 16
F32 = jnp.float32
BF16 = jnp.bfloat16
ZS = 8
CHUNKS = 4
Z_ORDER = (0, 1, 7, 2, 6, 3, 5, 4)
GROUPS = ((0, 6), (6, 10), (10, 14), (14, 16))
PLACE_GROUP = (0, 0, 0, 1, 1, 2, 2, 3)
Z_SENDS = (4, 3, 5, 2, 6, 1, 7)
XY_SENDS = sorted(
    ((dy, dx) for dy in range(4) for dx in range(4) if dy or dx),
    key=lambda t: -(min(t[0], 4 - t[0]) + min(t[1], 4 - t[1])),
)


def iota(shape, dim):
    return lax.broadcasted_iota(jnp.int32, shape, dim)


def dot(a, b):
    return jnp.dot(a, b, preferred_element_type=F32)


def dot_nt(a, b):
    return lax.dot_general(a, b, (((1,), (1,)), ((), ())), preferred_element_type=F32)


def wrap(i, n):
    return lax.rem(i + n, n)


def slot_plane(slot, z):
    place = slot // 2
    offset = jnp.zeros_like(slot)
    for k, dz in enumerate(Z_ORDER):
        offset = jnp.where(place == k, dz, offset)
    return ((z + offset) % ZS) * 2 + slot % 2


def choices(ids, pair_id, term_y):
    pick, term = [], []
    for j in range(MB):
        idj = ids[:, j : j + 1]
        pick.append(jnp.where(pair_id == idj, 1.0, 0.0).astype(BF16))
        term.append(jnp.where(term_y == idj % NY, 1.0, 0.0).astype(BF16))
    return jnp.concatenate(pick, axis=0), jnp.concatenate(term, axis=0)


def both_halves(block, rows):
    flat = block.reshape(QRY * 16, 128)
    raised = pltpu.roll(flat.astype(F32), QRY * 16 - rows, axis=0).astype(BF16)
    return jnp.concatenate([flat, raised], axis=1)


def choose_early(pick, near, mid):
    outs = jnp.concatenate(
        [
            both_halves(mid[0], 8),
            both_halves(mid[1], 8),
            jnp.concatenate([near[half].reshape(QRY * 16, 128) for half in range(2)], axis=1),
        ],
        axis=0,
    )
    return dot(pick, outs)


def merge(ids, chosen, pick, term, far, lane_z):
    rows = ids.shape[0]
    lse = dot(term, far.reshape(QRY * 16, 128))
    chosen = chosen + dot(pick, both_halves(far, 4))
    lses = []
    for j in range(MB):
        lj = jnp.where(lane_z == ids[:, j : j + 1] // NY, lse[j * rows : (j + 1) * rows], 0.0)
        for shift in (8, 16, 32, 64):
            lj = lj + pltpu.roll(lj, shift, axis=1)
        lses.append(lj)
    top = jnp.maximum(jnp.maximum(lses[0], lses[1]), jnp.maximum(lses[2], lses[3]))
    weights = [jnp.exp(lj - top) for lj in lses]
    inv = 1.0 / (weights[0] + weights[1] + weights[2] + weights[3])
    attn = jnp.zeros((rows, D), F32)
    for j in range(MB):
        wj = weights[j] * inv
        attn = attn + jnp.concatenate([wj, wj], axis=1) * chosen[j * rows : (j + 1) * rows]
    return attn


def kernel(
    feat_hbm, conv_hbm, queries_hbm, wq_hbm, wk_hbm, wv_hbm, wo_hbm, gain_hbm, mw_hbm, mb_hbm,
    embed_ref, logit_ref,
    ext, taps, qbuf, qpbuf, wq, wk, wv, wo, mw, gain, mb, wvp, wop, pix, pix_t, keys, vals,
    stage1, near, mid, far, state, acc, pick_all, term_all, woven,
    local_sem, conv_sem, halo_send, halo_recv, q_send, q_recv, p_send, p_recv,
    s_send, s_recv, y_send, y_recv, c_send, c_recv, entered,
):
    s = lax.axis_index("span")
    q = lax.axis_index("qry")
    z, core = s // 2, lax.rem(s, 2)
    y, x = q // 4, lax.rem(q, 4)
    up, down = wrap(s + 1, SPAN), wrap(s - 1, SPAN)
    right, left = wrap(q + 1, QRY), wrap(q - 1, QRY)
    z_peers = [(d, c) for d in Z_SENDS for c in range(2)] + [(0, 1)]
    z_index = [wrap(z + d, ZS) * 2 + (c if d else 1 - core) for d, c in z_peers]
    xy_index = [lax.rem(y + dy, 4) * 4 + lax.rem(x + dx, 4) for dy, dx in XY_SENDS]

    barrier = pltpu.get_barrier_semaphore()
    for d in (1, -1, 2, -2, 3, -3, 4, -4):
        pl.semaphore_signal(barrier, inc=1, device_id=(wrap(s + d, SPAN), q), device_id_type=MESH)
    for block in xy_index[::-1]:
        pl.semaphore_signal(barrier, inc=1, device_id=(s, block), device_id_type=MESH)

    own = pltpu.make_async_copy(feat_hbm.at[0], ext.at[1, pl.ds(1, 2)], local_sem.at[0])
    own.start()
    first_loads, loads = [], []
    for k, (src, dst) in enumerate(
        (
            (mb_hbm, mb),
            (queries_hbm, qbuf.at[q]),
            (wq_hbm, wq),
            (wv_hbm, wv),
            (wo_hbm, wo),
            (wk_hbm, wk),
            (mw_hbm, mw),
            (gain_hbm, gain),
        )
    ):
        copy = pltpu.make_async_copy(src, dst, local_sem.at[1 + k])
        copy.start()
        (first_loads if k < 3 else loads).append(copy)
    conv_loads = [
        pltpu.make_async_copy(conv_hbm.at[:, dx], taps.at[dx], conv_sem.at[dx]) for dx in range(3)
    ]
    for load in conv_loads:
        load.start()
    pl.semaphore_wait(barrier, 8 + len(xy_index))

    for k, d in enumerate((4, -4)):
        pl.semaphore_signal(entered.at[k], inc=1, device_id=(wrap(s + d, SPAN), q), device_id_type=MESH)

    sends = []

    def send(src, dst, k, peer):
        copy = pltpu.make_async_remote_copy(
            src_ref=src, dst_ref=dst, send_sem=halo_send.at[k], recv_sem=halo_recv.at[k],
            device_id=peer, device_id_type=MESH,
        )
        copy.start()
        sends.append(copy)
        return copy

    rows = feat_hbm.at[0]
    chunks = [pl.ds(k * (NX // CHUNKS), NX // CHUNKS) for k in range(CHUNKS)]
    across = []
    for k, chunk in enumerate(chunks):
        across.append(send(rows.at[1, chunk], ext.at[1, 0, chunk], 2 * k, (s, right)))
        across.append(send(rows.at[0, chunk], ext.at[1, 3, chunk], 2 * k + 1, (s, left)))
    from_down = send(rows, ext.at[0, pl.ds(1, 2)], 2 * CHUNKS, (up, q))
    from_up = send(rows, ext.at[2, pl.ds(1, 2)], 2 * CHUNKS + 1, (down, q))

    def to_plane(buf, send_sem, recv_sem):
        for block in xy_index:
            pltpu.make_async_remote_copy(
                src_ref=buf.at[q], dst_ref=buf.at[q], send_sem=send_sem, recv_sem=recv_sem,
                device_id=(s, block), device_id_type=MESH,
            ).start()

    def wait_slots(buf, count, sem):
        some = buf.at[pl.ds(0, count)]
        pltpu.make_async_copy(some, some, sem).wait()

    for load in first_loads:
        load.wait()
    qproj = (dot(qbuf[q].astype(BF16), wq[0]) * HEAD_DIM**-0.5).astype(BF16)
    qpbuf[q] = jnp.concatenate([qproj[:, 0:128], qproj[:, 128:256]], axis=0)
    to_plane(qpbuf, p_send, p_recv)

    perm = jnp.where(
        iota((D, D), 1) == (iota((D, D), 0) % HEAD_DIM) * HEADS + iota((D, D), 0) // HEAD_DIM, 1.0, 0.0
    ).astype(BF16)
    perm_t = jnp.where(
        iota((D, D), 0) == (iota((D, D), 1) % HEAD_DIM) * HEADS + iota((D, D), 1) // HEAD_DIM, 1.0, 0.0
    ).astype(BF16)
    for load in loads:
        load.wait()
    for layer in range(LAYERS):
        wvp[layer] = dot(wv[layer], perm).astype(BF16)
        wop[layer] = dot(perm_t, wo[layer]).astype(BF16)

    lists = mb[...]
    all_ids = lists.astype(F32).T.astype(jnp.int32)
    own_ids, picks, listed = [], [], []
    for r in range(2):
        block_id = s * NY + q * 2 + r
        listed.append(jnp.max(jnp.where(all_ids == block_id, 1, 0), axis=1, keepdims=True) > 0)
        picks.append(jnp.max(jnp.where(lists == block_id, 1.0, 0.0), axis=0, keepdims=True))
        own_ids.append(jnp.sum(jnp.where(listed[r], all_ids.astype(F32), 0.0), axis=0, keepdims=True))
    own_ids = jnp.concatenate(own_ids + [jnp.full((6, MB), -1.0, F32)], axis=0).astype(jnp.int32)
    picks = jnp.concatenate(picks + [jnp.zeros((6, NQ), F32)], axis=0).astype(BF16)

    col = iota((1, QRY * 64), 1)
    group, kind = col // 256, col % 16
    group = jnp.where(group == 3, 3, jnp.where(group == 2, 0, group + 1))
    width = jnp.where(group == 0, 8, jnp.where(group == 3, 2, 4))
    place = kind & (width - 1)
    half = (kind - place) // width
    pair_id = slot_plane(jnp.where(group == 0, 0, 2 + 4 * group) + place, z) * NY + ((col % 256) // 16) * 2 + half
    valid = jnp.where(half < 2, place, 8) < jnp.where(group == 0, 6, width)
    pair_id = jnp.where(valid, pair_id, -2)
    row = iota((1, QRY * 16), 1)
    kind = row % 16 - 8
    term_y = (row // 16) * 2 + jnp.where(kind < 3, 0, 1)
    term_y = jnp.where((kind >= 0) & (kind < 6), term_y, -2)
    lane_z = slot_plane(iota((1, 128), 1) // HEADS, z)
    own_pick, own_term = choices(own_ids, pair_id, term_y)
    pick_all[...], term_all[...] = choices(all_ids, pair_id, term_y)

    relays = []
    for k, copy in enumerate(across):
        copy.wait_recv()
        chunk, row = chunks[k // 2], 3 * (k % 2)
        first = 2 * CHUNKS + 2 + 2 * k
        relays.append(send(ext.at[1, row, chunk], ext.at[0, row, chunk], first, (up, q)))
        relays.append(send(ext.at[1, row, chunk], ext.at[2, row, chunk], first + 1, (down, q)))
    to_plane(qbuf, q_send, q_recv)
    own.wait()
    for load in conv_loads:
        load.wait()

    middle = [ext[1, row] for row in range(4)]
    middle[0] = jnp.where(q > 0, middle[0], jnp.zeros_like(middle[0]))
    middle[3] = jnp.where(q < QRY - 1, middle[3], jnp.zeros_like(middle[3]))
    slab = jnp.concatenate(
        [jnp.concatenate(middle[dy : dy + 2], axis=0) for dy in range(3)], axis=1
    )
    for dx in range(3):
        acc[dx] = dot(slab, taps[dx, 3:6].reshape(3 * D, D))
    for dz, copy, outside in ((0, from_down, s == 0), (2, from_up, s == SPAN - 1)):
        copy.wait_recv()

        @pl.when(outside)
        def _():
            ext[dz, 1:3] = jnp.zeros((2, NX, D), BF16)

        pair = jnp.concatenate([ext[dz, 1], ext[dz, 2]], axis=1)
        for dx in range(3):
            for r in range(2):
                weights = taps[dx, 3 * dz + 1 - r : 3 * dz + 3 - r].reshape(2 * D, D)
                acc[dx, r * NX : (r + 1) * NX] += dot(pair, weights)

    for copy in relays:
        copy.wait_recv()

    @pl.when((s == 0) | (q == 0))
    def _():
        ext[0, 0] = jnp.zeros((NX, D), BF16)

    @pl.when((s == 0) | (q == QRY - 1))
    def _():
        ext[0, 3] = jnp.zeros((NX, D), BF16)

    @pl.when((s == SPAN - 1) | (q == 0))
    def _():
        ext[2, 0] = jnp.zeros((NX, D), BF16)

    @pl.when((s == SPAN - 1) | (q == QRY - 1))
    def _():
        ext[2, 3] = jnp.zeros((NX, D), BF16)

    def column(dx):
        parts = []
        for r in range(2):
            corner = jnp.concatenate([ext[0, 3 * r], ext[2, 3 * r]], axis=1)
            weights = jnp.concatenate([taps[dx, 2 * r], taps[dx, 6 + 2 * r]], axis=0)
            parts.append(acc[dx, r * NX : (r + 1) * NX] + dot(corner, weights))
        return jnp.concatenate(parts, axis=0)

    x_at = iota((2 * NX, D), 0) % NX
    conv = jnp.where(x_at == 0, 0.0, pltpu.roll(column(0), 1, axis=0))
    conv = conv + column(1)
    conv = conv + jnp.where(x_at == NX - 1, 0.0, pltpu.roll(column(2), 2 * NX - 1, axis=0))
    pixel = jnp.maximum(conv, 0.0).astype(BF16)
    pix[...] = pixel
    keys[0] = dot(pixel, wk[0]).astype(BF16)
    vals[0] = dot(pixel, wvp[0]).astype(BF16)

    wait_slots(qpbuf, QRY - 1, p_recv)
    projected = jnp.concatenate(
        [qpbuf[:, half * 8 : half * 8 + 8, :].astype(F32).reshape(NQ, 128) for half in range(2)], axis=1
    )
    qproj = dot(picks, projected.astype(BF16))

    head_of = iota((HEADS, D), 1) // HEAD_DIM == iota((HEADS, D), 0)
    head_of_lane = iota((HEADS, D), 1) % HEADS == iota((HEADS, D), 0)
    lse_lane = iota((HEADS, 128), 1) % HEADS == iota((HEADS, 128), 0)
    for k in range(2):
        pl.semaphore_wait(entered.at[k], 1)
    for layer in range(LAYERS):
        spread = jnp.concatenate(
            [jnp.where(head_of, qproj[r : r + 1], 0.0) for r in range(2)], axis=0
        ).astype(BF16)
        scores = dot_nt(spread, keys[0]) if layer == 0 else dot(spread, keys[1])
        scores = jnp.concatenate([scores[0:8, 0:NX], scores[8:16, NX : 2 * NX]], axis=0)
        top = jnp.max(scores, axis=1, keepdims=True)
        prob = jnp.exp(scores - top)
        total = jnp.sum(prob, axis=1, keepdims=True)
        inv = 1.0 / total
        lse = top + jnp.log(total)
        prob = prob.astype(BF16)
        low, high, lines = [], [], []
        for r in range(2):
            part = slice(r * HEADS, (r + 1) * HEADS)
            weighted = dot(prob[part], vals[layer, r * NX : (r + 1) * NX])
            out = jnp.sum(jnp.where(head_of_lane, weighted * inv[part], 0.0), axis=0, keepdims=True)
            low.append(out[:, 0:128])
            high.append(out[:, 128:256])
            lines.append(jnp.sum(jnp.where(lse_lane, lse[part], 0.0), axis=0, keepdims=True))
        buf = stage1.at[layer]
        buf[core] = jnp.concatenate(low + high + lines + [jnp.zeros((2, 128), F32)], axis=0)
        for (d, c), plane in zip(z_peers, z_index):
            place = Z_ORDER.index((ZS - d) % ZS)
            pltpu.make_async_remote_copy(
                src_ref=buf.at[core], dst_ref=buf.at[place * 2 + core],
                send_sem=s_send.at[layer], recv_sem=s_recv.at[layer, PLACE_GROUP[place]],
                device_id=(plane, q), device_id_type=MESH,
            ).start()
        if layer == 0:
            keys[1] = dot(pix[...], wk[1]).T.astype(BF16)
            pix_t[...] = pix[...].astype(F32).T.astype(BF16)
            vals[1] = dot(pix[...], wvp[1]).astype(BF16)
        lines = [jnp.zeros((1, 128), F32)] * 2
        for group, (start, end) in enumerate(GROUPS):
            count = end - start
            wait_slots(buf, count - (group == 0), s_recv.at[layer, group])
            got = stage1[layer, start:end]
            parts = [got[:, k, :] for k in range(4)]
            own_lanes = iota((count, 128), 1) // HEADS == start + iota((count, 128), 0)
            for r in range(2):
                kept = jnp.where(own_lanes, got[:, 4 + r, :], 0.0)
                lines[r] = lines[r] + jnp.sum(kept, axis=0, keepdims=True)
            if group == 0:
                blank = jnp.zeros((2, 128), F32)
                halves = [
                    jnp.concatenate([parts[2 * k], blank, parts[2 * k + 1], blank], axis=0) for k in range(2)
                ]
                near[layer, core, q] = jnp.where(core == 0, halves[0], halves[1]).astype(BF16)
                to_plane(near.at[layer, core], y_send.at[layer, 0], y_recv.at[layer, 0])
            elif group < 3:
                mid[layer, group - 1, q] = jnp.concatenate(parts, axis=0).astype(BF16)
                to_plane(mid.at[layer, group - 1], y_send.at[layer, group], y_recv.at[layer, group])
        message = parts
        for line in lines:
            for _ in range(3):
                term = line.astype(BF16).astype(F32)
                message.append(term)
                line = line - term
        message.append(jnp.zeros((2, 128), F32))
        far[layer, q] = jnp.concatenate(message, axis=0).astype(BF16)
        to_plane(far.at[layer], y_send.at[layer, 3], y_recv.at[layer, 3])
        if layer == 1:
            chosen = choose_early(pick_all[:, : QRY * 48], near[0], mid[0])
            attn = merge(all_ids, chosen, pick_all[:, QRY * 48 :], term_all[...], far[0], lane_z)
            state[...] = qbuf[...].reshape(NQ, D) + dot(attn.astype(BF16), wop[0])
        if layer == 0:
            wait_slots(qbuf, QRY - 1, q_recv)
            state_all = qbuf[...].reshape(NQ, D)
            own_state = [
                jnp.sum(jnp.where(listed[r], state_all, 0.0), axis=0, keepdims=True) for r in range(2)
            ]
            own_state = jnp.concatenate(own_state + [jnp.zeros((6, D), F32)], axis=0)
        wait_slots(near.at[layer, 0], QRY - 1, y_recv.at[layer, 0])
        swap = pltpu.make_async_remote_copy(
            src_ref=near.at[layer, core], dst_ref=near.at[layer, core],
            send_sem=c_send.at[layer], recv_sem=c_recv.at[layer],
            device_id=(z * 2 + 1 - core, q), device_id_type=MESH,
        )
        swap.start()
        sends.append(swap)
        for k in range(2):
            wait_slots(mid.at[layer, k], QRY - 1, y_recv.at[layer, 1 + k])
        swap.wait_recv()
        early = own_pick[:, : QRY * 48] if layer == 0 else pick_all[:, : QRY * 48]
        chosen = choose_early(early, near[layer], mid[layer])
        wait_slots(far.at[layer], QRY - 1, y_recv.at[layer, 3])
        if layer == 0:
            attn = merge(own_ids, chosen, own_pick[:, QRY * 48 :], own_term, far[0], lane_z)
            own_state = own_state + dot(attn.astype(BF16), wop[0])
            qproj = (dot(own_state.astype(BF16), wq[1]) * HEAD_DIM**-0.5).astype(BF16).astype(F32)

    attn = merge(all_ids, chosen, pick_all[:, QRY * 48 :], term_all[...], far[1], lane_z)
    final = state[...] + dot(attn.astype(BF16), wop[1])
    mean = jnp.mean(final, axis=-1, keepdims=True)
    centered = final - mean
    var = jnp.mean(centered * centered, axis=-1, keepdims=True)
    embed = centered * lax.rsqrt(var + 1e-05) * gain[...]
    state[...] = embed
    embed_ref[...] = state[pl.ds(pl.multiple_of(q * 8, 8), 8), :]
    mask_embed = dot(embed.astype(BF16), mw[...]).astype(BF16)
    logits = dot(mask_embed, pix_t[...]) * D**-0.5
    for r in range(2):
        woven[pl.ds(r, NQ, stride=2), :] = logits[:, r * NX : (r + 1) * NX]
    logit_ref[...] = woven[...].astype(BF16)

    for copy in sends:
        copy.wait_send()
    wait_slots(qbuf, QRY - 1, q_send)
    wait_slots(qpbuf, QRY - 1, p_send)
    for layer in range(LAYERS):
        wait_slots(stage1.at[layer], SPAN - 1, s_send.at[layer])
        wait_slots(near.at[layer, 0], QRY - 1, y_send.at[layer, 0])
        for k in range(2):
            wait_slots(mid.at[layer, k], QRY - 1, y_send.at[layer, 1 + k])
        wait_slots(far.at[layer], QRY - 1, y_send.at[layer, 3])


def hand_over(embed_ref, logit_ref, embed_out, logit_out, sem):
    copies = [
        pltpu.make_async_copy(logit_ref, logit_out, sem.at[0]),
        pltpu.make_async_copy(embed_ref, embed_out, sem.at[1]),
    ]
    for copy in copies:
        copy.start()
    for copy in copies:
        copy.wait()


def local(
    features, conv_weight, queries, w_query, w_key, w_value, w_out, norm_gain, mask_weight, mask_blocks
):
    hbm = pl.BlockSpec(memory_space=pltpu.HBM)
    vmem = pl.BlockSpec(memory_space=pltpu.VMEM)
    dma = pltpu.SemaphoreType.DMA
    square = pltpu.VMEM((LAYERS, D, D), BF16)
    embed, logits = pl.pallas_call(
        kernel,
        out_shape=(
            jax.ShapeDtypeStruct((8, D), F32),
            jax.ShapeDtypeStruct((2 * NQ, NX), BF16),
        ),
        in_specs=[hbm] * 10,
        out_specs=(vmem, vmem),
        scratch_shapes=[
            pltpu.VMEM((3, 4, NX, D), BF16),
            pltpu.VMEM((3, 9, D, D), BF16),
            pltpu.VMEM((QRY, 8, D), F32),
            pltpu.VMEM((QRY, 16, 128), BF16),
            square,
            square,
            square,
            square,
            pltpu.VMEM((D, D), BF16),
            pltpu.VMEM((1, D), F32),
            pltpu.VMEM((MB, NQ), jnp.int32),
            square,
            square,
            pltpu.VMEM((2 * NX, D), BF16),
            pltpu.VMEM((D, 2 * NX), BF16),
            square,
            square,
            pltpu.VMEM((LAYERS, SPAN, 8, 128), F32),
            pltpu.VMEM((LAYERS, 2, QRY, 16, 128), BF16),
            pltpu.VMEM((LAYERS, 2, QRY, 16, 128), BF16),
            pltpu.VMEM((LAYERS, QRY, 16, 128), BF16),
            pltpu.VMEM((NQ, D), F32),
            pltpu.VMEM((3, 2 * NX, D), F32),
            pltpu.VMEM((MB * NQ, QRY * 64), BF16),
            pltpu.VMEM((MB * NQ, QRY * 16), BF16),
            pltpu.VMEM((2 * NQ, NX), F32),
            dma((9,)),
            dma((3,)),
            dma((6 * CHUNKS + 2,)),
            dma((6 * CHUNKS + 2,)),
            dma,
            dma,
            dma,
            dma,
            dma((LAYERS,)),
            dma((LAYERS, 4)),
            dma((LAYERS, 4)),
            dma((LAYERS, 4)),
            dma((LAYERS,)),
            dma((LAYERS,)),
            pltpu.SemaphoreType.REGULAR((2,)),
        ],
        compiler_params=pltpu.CompilerParams(
            collective_id=0, has_side_effects=True, vmem_limit_bytes=40 * 1024 * 1024
        ),
    )(
        *(
            pltpu.with_memory_space_constraint(operand, pltpu.HBM)
            for operand in (
                features,
                conv_weight.reshape(9, 3, D, D),
                queries,
                w_query,
                w_key,
                w_value,
                w_out,
                norm_gain.reshape(1, D),
                mask_weight,
                mask_blocks.T,
            )
        )
    )
    embed, logits = pl.pallas_call(
        hand_over,
        out_shape=(
            jax.ShapeDtypeStruct((8, D), F32),
            jax.ShapeDtypeStruct((2 * NQ, NX), BF16),
        ),
        in_specs=[vmem] * 2,
        out_specs=(pl.BlockSpec(memory_space=pl.ANY),) * 2,
        scratch_shapes=[dma((2,))],
    )(*(pltpu.with_memory_space_constraint(part, pltpu.VMEM) for part in (embed, logits)))
    return embed, logits.reshape(NQ, 1, 2, NX)


def solution(mesh):
    return jax.shard_map(
        local,
        mesh=mesh,
        in_specs=(
            P("span", "qry", None, None),
            P(),
            P("qry", None),
            P(),
            P(),
            P(),
            P(),
            P(),
            P(),
            P(),
        ),
        out_specs=(P("qry", None), P(None, "span", "qry", None)),
        check_vma=False,
    )
```

```python
import jax
import jax.numpy as jnp
from jax import lax
from jax.experimental import pallas as pl
from jax.experimental.pallas import tpu as pltpu
from jax.sharding import PartitionSpec as P

MESH = pl.DeviceIdType.MESH
HEADS = 8
LAYERS = 2
D = 256
HEAD_DIM = 32
NX = 128
NQ = 128
MB = 4
NY = 32
SPAN = 16
QRY = 16
F32 = jnp.float32
BF16 = jnp.bfloat16
ZS = 8
CHUNKS = 4
Z_ORDER = (0, 1, 7, 2, 6, 3, 5, 4)
GROUPS = ((0, 6), (6, 10), (10, 14), (14, 16))
PLACE_GROUP = (0, 0, 0, 1, 1, 2, 2, 3)
Z_SENDS = (4, 3, 5, 2, 6, 1, 7)
XY_SENDS = sorted(
    ((dy, dx) for dy in range(4) for dx in range(4) if dy or dx),
    key=lambda t: -(min(t[0], 4 - t[0]) * 10 + min(t[1], 4 - t[1]) * 11),
)


def iota(shape, dim):
    return lax.broadcasted_iota(jnp.int32, shape, dim)


def dot(a, b):
    return jnp.dot(a, b, preferred_element_type=F32)


def dot_nt(a, b):
    return lax.dot_general(a, b, (((1,), (1,)), ((), ())), preferred_element_type=F32)


def wrap(i, n):
    return lax.rem(i + n, n)


def slot_plane(slot, z):
    place = slot // 2
    offset = jnp.zeros_like(slot)
    for k, dz in enumerate(Z_ORDER):
        offset = jnp.where(place == k, dz, offset)
    return ((z + offset) % ZS) * 2 + slot % 2


def choices(ids, pair_id, term_y):
    pick, term = [], []
    for j in range(MB):
        idj = ids[:, j : j + 1]
        pick.append(jnp.where(pair_id == idj, 1.0, 0.0).astype(BF16))
        term.append(jnp.where(term_y == idj % NY, 1.0, 0.0).astype(BF16))
    return jnp.concatenate(pick, axis=0), jnp.concatenate(term, axis=0)


def both_halves(block, rows):
    flat = block.reshape(QRY * 16, 128)
    raised = pltpu.roll(flat.astype(F32), QRY * 16 - rows, axis=0).astype(BF16)
    return jnp.concatenate([flat, raised], axis=1)


def choose_early(pick, near, mid):
    outs = jnp.concatenate(
        [
            both_halves(mid[0], 8),
            both_halves(mid[1], 8),
            jnp.concatenate([near[half].reshape(QRY * 16, 128) for half in range(2)], axis=1),
        ],
        axis=0,
    )
    return dot(pick, outs)


def merge(ids, chosen, pick, term, far, lane_z):
    rows = ids.shape[0]
    lse = dot(term, far.reshape(QRY * 16, 128))
    chosen = chosen + dot(pick, both_halves(far, 4))
    lses = []
    for j in range(MB):
        lj = jnp.where(lane_z == ids[:, j : j + 1] // NY, lse[j * rows : (j + 1) * rows], 0.0)
        for shift in (8, 16, 32, 64):
            lj = lj + pltpu.roll(lj, shift, axis=1)
        lses.append(lj)
    top = jnp.maximum(jnp.maximum(lses[0], lses[1]), jnp.maximum(lses[2], lses[3]))
    weights = [jnp.exp(lj - top) for lj in lses]
    inv = 1.0 / (weights[0] + weights[1] + weights[2] + weights[3])
    attn = jnp.zeros((rows, D), F32)
    for j in range(MB):
        wj = weights[j] * inv
        attn = attn + jnp.concatenate([wj, wj], axis=1) * chosen[j * rows : (j + 1) * rows]
    return attn


def kernel(
    feat_hbm, conv_hbm, queries_hbm, wq_hbm, wk_hbm, wv_hbm, wo_hbm, gain_hbm, mw_hbm, mb_hbm,
    embed_ref, logit_ref,
    ext, taps, qbuf, qpbuf, wq, wk, wv, wo, mw, gain, mb, wvp, wop, pix, pix_t, keys, vals,
    stage1, near, mid, far, state, acc, pick_all, term_all, woven,
    local_sem, conv_sem, halo_send, halo_recv, q_send, q_recv, p_send, p_recv,
    s_send, s_recv, y_send, y_recv, c_send, c_recv, entered,
):
    s = lax.axis_index("span")
    q = lax.axis_index("qry")
    z, core = s // 2, lax.rem(s, 2)
    y, x = q // 4, lax.rem(q, 4)
    up, down = wrap(s + 1, SPAN), wrap(s - 1, SPAN)
    right, left = wrap(q + 1, QRY), wrap(q - 1, QRY)
    z_peers = [(d, c) for d in Z_SENDS for c in range(2)] + [(0, 1)]
    z_index = [wrap(z + d, ZS) * 2 + (c if d else 1 - core) for d, c in z_peers]
    xy_index = [lax.rem(y + dy, 4) * 4 + lax.rem(x + dx, 4) for dy, dx in XY_SENDS]

    barrier = pltpu.get_barrier_semaphore()
    for d in (1, -1, 2, -2, 3, -3, 4, -4):
        pl.semaphore_signal(barrier, inc=1, device_id=(wrap(s + d, SPAN), q), device_id_type=MESH)
    for block in xy_index[::-1]:
        pl.semaphore_signal(barrier, inc=1, device_id=(s, block), device_id_type=MESH)

    own = pltpu.make_async_copy(feat_hbm.at[0], ext.at[1, pl.ds(1, 2)], local_sem.at[0])
    own.start()
    first_loads, loads = [], []
    for k, (src, dst) in enumerate(
        (
            (mb_hbm, mb),
            (queries_hbm, qbuf.at[q]),
            (wq_hbm, wq),
            (wv_hbm, wv),
            (wo_hbm, wo),
            (wk_hbm, wk),
            (mw_hbm, mw),
            (gain_hbm, gain),
        )
    ):
        copy = pltpu.make_async_copy(src, dst, local_sem.at[1 + k])
        copy.start()
        (first_loads if k < 3 else loads).append(copy)
    conv_loads = [
        pltpu.make_async_copy(conv_hbm.at[:, dx], taps.at[dx], conv_sem.at[dx]) for dx in range(3)
    ]
    for load in conv_loads:
        load.start()
    pl.semaphore_wait(barrier, 8 + len(xy_index))

    for k, d in enumerate((4, -4)):
        pl.semaphore_signal(entered.at[k], inc=1, device_id=(wrap(s + d, SPAN), q), device_id_type=MESH)

    sends = []

    def send(src, dst, k, peer):
        copy = pltpu.make_async_remote_copy(
            src_ref=src, dst_ref=dst, send_sem=halo_send.at[k], recv_sem=halo_recv.at[k],
            device_id=peer, device_id_type=MESH,
        )
        copy.start()
        sends.append(copy)
        return copy

    rows = feat_hbm.at[0]
    chunks = [pl.ds(k * (NX // CHUNKS), NX // CHUNKS) for k in range(CHUNKS)]
    across = []
    for k, chunk in enumerate(chunks):
        across.append(send(rows.at[1, chunk], ext.at[1, 0, chunk], 2 * k, (s, right)))
        across.append(send(rows.at[0, chunk], ext.at[1, 3, chunk], 2 * k + 1, (s, left)))
    from_down = send(rows, ext.at[0, pl.ds(1, 2)], 2 * CHUNKS, (up, q))
    from_up = send(rows, ext.at[2, pl.ds(1, 2)], 2 * CHUNKS + 1, (down, q))

    def to_plane(buf, send_sem, recv_sem):
        for block in xy_index:
            pltpu.make_async_remote_copy(
                src_ref=buf.at[q], dst_ref=buf.at[q], send_sem=send_sem, recv_sem=recv_sem,
                device_id=(s, block), device_id_type=MESH,
            ).start()

    def wait_slots(buf, count, sem):
        some = buf.at[pl.ds(0, count)]
        pltpu.make_async_copy(some, some, sem).wait()

    for load in first_loads:
        load.wait()
    qproj = (dot(qbuf[q].astype(BF16), wq[0]) * HEAD_DIM**-0.5).astype(BF16)
    qpbuf[q] = jnp.concatenate([qproj[:, 0:128], qproj[:, 128:256]], axis=0)
    to_plane(qpbuf, p_send, p_recv)

    perm = jnp.where(
        iota((D, D), 1) == (iota((D, D), 0) % HEAD_DIM) * HEADS + iota((D, D), 0) // HEAD_DIM, 1.0, 0.0
    ).astype(BF16)
    perm_t = jnp.where(
        iota((D, D), 0) == (iota((D, D), 1) % HEAD_DIM) * HEADS + iota((D, D), 1) // HEAD_DIM, 1.0, 0.0
    ).astype(BF16)
    for load in loads:
        load.wait()
    for layer in range(LAYERS):
        wvp[layer] = dot(wv[layer], perm).astype(BF16)
        wop[layer] = dot(perm_t, wo[layer]).astype(BF16)

    lists = mb[...]
    all_ids = lists.astype(F32).T.astype(jnp.int32)
    own_ids, picks, listed = [], [], []
    for r in range(2):
        block_id = s * NY + q * 2 + r
        listed.append(jnp.max(jnp.where(all_ids == block_id, 1, 0), axis=1, keepdims=True) > 0)
        picks.append(jnp.max(jnp.where(lists == block_id, 1.0, 0.0), axis=0, keepdims=True))
        own_ids.append(jnp.sum(jnp.where(listed[r], all_ids.astype(F32), 0.0), axis=0, keepdims=True))
    own_ids = jnp.concatenate(own_ids + [jnp.full((6, MB), -1.0, F32)], axis=0).astype(jnp.int32)
    picks = jnp.concatenate(picks + [jnp.zeros((6, NQ), F32)], axis=0).astype(BF16)

    col = iota((1, QRY * 64), 1)
    group, kind = col // 256, col % 16
    group = jnp.where(group == 3, 3, jnp.where(group == 2, 0, group + 1))
    width = jnp.where(group == 0, 8, jnp.where(group == 3, 2, 4))
    place = kind & (width - 1)
    half = (kind - place) // width
    pair_id = slot_plane(jnp.where(group == 0, 0, 2 + 4 * group) + place, z) * NY + ((col % 256) // 16) * 2 + half
    valid = jnp.where(half < 2, place, 8) < jnp.where(group == 0, 6, width)
    pair_id = jnp.where(valid, pair_id, -2)
    row = iota((1, QRY * 16), 1)
    kind = row % 16 - 8
    term_y = (row // 16) * 2 + jnp.where(kind < 3, 0, 1)
    term_y = jnp.where((kind >= 0) & (kind < 6), term_y, -2)
    lane_z = slot_plane(iota((1, 128), 1) // HEADS, z)
    own_pick, own_term = choices(own_ids, pair_id, term_y)

    relays = []
    for k, copy in enumerate(across):
        copy.wait_recv()
        chunk, row = chunks[k // 2], 3 * (k % 2)
        first = 2 * CHUNKS + 2 + 2 * k
        relays.append(send(ext.at[1, row, chunk], ext.at[0, row, chunk], first, (up, q)))
        relays.append(send(ext.at[1, row, chunk], ext.at[2, row, chunk], first + 1, (down, q)))
    own.wait()
    for load in conv_loads:
        load.wait()

    middle = [ext[1, row] for row in range(4)]
    middle[0] = jnp.where(q > 0, middle[0], jnp.zeros_like(middle[0]))
    middle[3] = jnp.where(q < QRY - 1, middle[3], jnp.zeros_like(middle[3]))
    slab = jnp.concatenate(
        [jnp.concatenate(middle[dy : dy + 2], axis=0) for dy in range(3)], axis=1
    )
    for dx in range(3):
        acc[dx] = dot(slab, taps[dx, 3:6].reshape(3 * D, D))
    for dz, copy, outside in ((0, from_down, s == 0), (2, from_up, s == SPAN - 1)):
        copy.wait_recv()

        @pl.when(outside)
        def _():
            ext[dz, 1:3] = jnp.zeros((2, NX, D), BF16)

        pair = jnp.concatenate([ext[dz, 1], ext[dz, 2]], axis=1)
        for dx in range(3):
            for r in range(2):
                weights = taps[dx, 3 * dz + 1 - r : 3 * dz + 3 - r].reshape(2 * D, D)
                acc[dx, r * NX : (r + 1) * NX] += dot(pair, weights)

    for copy in relays:
        copy.wait_recv()

    @pl.when((s == 0) | (q == 0))
    def _():
        ext[0, 0] = jnp.zeros((NX, D), BF16)

    @pl.when((s == 0) | (q == QRY - 1))
    def _():
        ext[0, 3] = jnp.zeros((NX, D), BF16)

    @pl.when((s == SPAN - 1) | (q == 0))
    def _():
        ext[2, 0] = jnp.zeros((NX, D), BF16)

    @pl.when((s == SPAN - 1) | (q == QRY - 1))
    def _():
        ext[2, 3] = jnp.zeros((NX, D), BF16)

    def column(dx):
        parts = []
        for r in range(2):
            corner = jnp.concatenate([ext[0, 3 * r], ext[2, 3 * r]], axis=1)
            weights = jnp.concatenate([taps[dx, 2 * r], taps[dx, 6 + 2 * r]], axis=0)
            parts.append(acc[dx, r * NX : (r + 1) * NX] + dot(corner, weights))
        return jnp.concatenate(parts, axis=0)

    x_at = iota((2 * NX, D), 0) % NX
    conv = jnp.where(x_at == 0, 0.0, pltpu.roll(column(0), 1, axis=0))
    conv = conv + column(1)
    conv = conv + jnp.where(x_at == NX - 1, 0.0, pltpu.roll(column(2), 2 * NX - 1, axis=0))
    pixel = jnp.maximum(conv, 0.0).astype(BF16)
    pix[...] = pixel
    keys[0] = dot(pixel, wk[0]).astype(BF16)
    vals[0] = dot(pixel, wvp[0]).astype(BF16)

    wait_slots(qpbuf, QRY - 1, p_recv)
    projected = jnp.concatenate(
        [qpbuf[:, half * 8 : half * 8 + 8, :].astype(F32).reshape(NQ, 128) for half in range(2)], axis=1
    )
    qproj = dot(picks, projected.astype(BF16))

    head_of = iota((HEADS, D), 1) // HEAD_DIM == iota((HEADS, D), 0)
    head_of_lane = iota((HEADS, D), 1) % HEADS == iota((HEADS, D), 0)
    lse_lane = iota((HEADS, 128), 1) % HEADS == iota((HEADS, 128), 0)
    for k in range(2):
        pl.semaphore_wait(entered.at[k], 1)
    for layer in range(LAYERS):
        spread = jnp.concatenate(
            [jnp.where(head_of, qproj[r : r + 1], 0.0) for r in range(2)], axis=0
        ).astype(BF16)
        scores = dot_nt(spread, keys[0]) if layer == 0 else dot(spread, keys[1])
        scores = jnp.concatenate([scores[0:8, 0:NX], scores[8:16, NX : 2 * NX]], axis=0)
        top = jnp.max(scores, axis=1, keepdims=True)
        prob = jnp.exp(scores - top)
        total = jnp.sum(prob, axis=1, keepdims=True)
        inv = 1.0 / total
        lse = top + jnp.log(total)
        prob = prob.astype(BF16)
        low, high, lines = [], [], []
        for r in range(2):
            part = slice(r * HEADS, (r + 1) * HEADS)
            weighted = dot(prob[part], vals[layer, r * NX : (r + 1) * NX])
            out = jnp.sum(jnp.where(head_of_lane, weighted * inv[part], 0.0), axis=0, keepdims=True)
            low.append(out[:, 0:128])
            high.append(out[:, 128:256])
            lines.append(jnp.sum(jnp.where(lse_lane, lse[part], 0.0), axis=0, keepdims=True))
        buf = stage1.at[layer]
        buf[core] = jnp.concatenate(low + high + lines + [jnp.zeros((2, 128), F32)], axis=0)
        for (d, c), plane in zip(z_peers, z_index):
            place = Z_ORDER.index((ZS - d) % ZS)
            pltpu.make_async_remote_copy(
                src_ref=buf.at[core], dst_ref=buf.at[place * 2 + core],
                send_sem=s_send.at[layer], recv_sem=s_recv.at[layer, PLACE_GROUP[place]],
                device_id=(plane, q), device_id_type=MESH,
            ).start()
        if layer == 0:
            to_plane(qbuf, q_send, q_recv)
            keys[1] = dot(pix[...], wk[1]).T.astype(BF16)
            pix_t[...] = pix[...].astype(F32).T.astype(BF16)
            vals[1] = dot(pix[...], wvp[1]).astype(BF16)
            pick_all[...], term_all[...] = choices(all_ids, pair_id, term_y)
        else:
            chosen = choose_early(pick_all[:, : QRY * 48], near[0], mid[0])
            attn = merge(all_ids, chosen, pick_all[:, QRY * 48 :], term_all[...], far[0], lane_z)
            state[...] = qbuf[...].reshape(NQ, D) + dot(attn.astype(BF16), wop[0])
        lines = [jnp.zeros((1, 128), F32)] * 2
        for group, (start, end) in enumerate(GROUPS):
            count = end - start
            wait_slots(buf, count - (group == 0), s_recv.at[layer, group])
            got = stage1[layer, start:end]
            parts = [got[:, k, :] for k in range(4)]
            own_lanes = iota((count, 128), 1) // HEADS == start + iota((count, 128), 0)
            for r in range(2):
                kept = jnp.where(own_lanes, got[:, 4 + r, :], 0.0)
                lines[r] = lines[r] + jnp.sum(kept, axis=0, keepdims=True)
            if group == 0:
                blank = jnp.zeros((2, 128), F32)
                halves = [
                    jnp.concatenate([parts[2 * k], blank, parts[2 * k + 1], blank], axis=0) for k in range(2)
                ]
                near[layer, core, q] = jnp.where(core == 0, halves[0], halves[1]).astype(BF16)
                to_plane(near.at[layer, core], y_send.at[layer, 0], y_recv.at[layer, 0])
            elif group < 3:
                mid[layer, group - 1, q] = jnp.concatenate(parts, axis=0).astype(BF16)
                to_plane(mid.at[layer, group - 1], y_send.at[layer, group], y_recv.at[layer, group])
        message = parts
        for line in lines:
            for _ in range(3):
                term = line.astype(BF16).astype(F32)
                message.append(term)
                line = line - term
        message.append(jnp.zeros((2, 128), F32))
        far[layer, q] = jnp.concatenate(message, axis=0).astype(BF16)
        to_plane(far.at[layer], y_send.at[layer, 3], y_recv.at[layer, 3])
        if layer == 0:
            wait_slots(qbuf, QRY - 1, q_recv)
            state_all = qbuf[...].reshape(NQ, D)
            own_state = [
                jnp.sum(jnp.where(listed[r], state_all, 0.0), axis=0, keepdims=True) for r in range(2)
            ]
            own_state = jnp.concatenate(own_state + [jnp.zeros((6, D), F32)], axis=0)
        wait_slots(near.at[layer, 0], QRY - 1, y_recv.at[layer, 0])
        swap = pltpu.make_async_remote_copy(
            src_ref=near.at[layer, core], dst_ref=near.at[layer, core],
            send_sem=c_send.at[layer], recv_sem=c_recv.at[layer],
            device_id=(z * 2 + 1 - core, q), device_id_type=MESH,
        )
        swap.start()
        sends.append(swap)
        for k in range(2):
            wait_slots(mid.at[layer, k], QRY - 1, y_recv.at[layer, 1 + k])
        swap.wait_recv()
        early = own_pick[:, : QRY * 48] if layer == 0 else pick_all[:, : QRY * 48]
        chosen = choose_early(early, near[layer], mid[layer])
        wait_slots(far.at[layer], QRY - 1, y_recv.at[layer, 3])
        if layer == 0:
            attn = merge(own_ids, chosen, own_pick[:, QRY * 48 :], own_term, far[0], lane_z)
            own_state = own_state + dot(attn.astype(BF16), wop[0])
            qproj = (dot(own_state.astype(BF16), wq[1]) * HEAD_DIM**-0.5).astype(BF16).astype(F32)

    attn = merge(all_ids, chosen, pick_all[:, QRY * 48 :], term_all[...], far[1], lane_z)
    final = state[...] + dot(attn.astype(BF16), wop[1])
    mean = jnp.mean(final, axis=-1, keepdims=True)
    centered = final - mean
    var = jnp.mean(centered * centered, axis=-1, keepdims=True)
    embed = centered * lax.rsqrt(var + 1e-05) * gain[...]
    state[...] = embed
    embed_ref[...] = state[pl.ds(pl.multiple_of(q * 8, 8), 8), :]
    mask_embed = dot(embed.astype(BF16), mw[...]).astype(BF16)
    logits = dot(mask_embed, pix_t[...]) * D**-0.5
    for r in range(2):
        woven[pl.ds(r, NQ, stride=2), :] = logits[:, r * NX : (r + 1) * NX]
    logit_ref[...] = woven[...].astype(BF16)

    for copy in sends:
        copy.wait_send()
    wait_slots(qbuf, QRY - 1, q_send)
    wait_slots(qpbuf, QRY - 1, p_send)
    for layer in range(LAYERS):
        wait_slots(stage1.at[layer], SPAN - 1, s_send.at[layer])
        wait_slots(near.at[layer, 0], QRY - 1, y_send.at[layer, 0])
        for k in range(2):
            wait_slots(mid.at[layer, k], QRY - 1, y_send.at[layer, 1 + k])
        wait_slots(far.at[layer], QRY - 1, y_send.at[layer, 3])


def hand_over(embed_ref, logit_ref, embed_out, logit_out, sem):
    copies = [
        pltpu.make_async_copy(logit_ref, logit_out, sem.at[0]),
        pltpu.make_async_copy(embed_ref, embed_out, sem.at[1]),
    ]
    for copy in copies:
        copy.start()
    for copy in copies:
        copy.wait()


def local(
    features, conv_weight, queries, w_query, w_key, w_value, w_out, norm_gain, mask_weight, mask_blocks
):
    hbm = pl.BlockSpec(memory_space=pltpu.HBM)
    vmem = pl.BlockSpec(memory_space=pltpu.VMEM)
    dma = pltpu.SemaphoreType.DMA
    square = pltpu.VMEM((LAYERS, D, D), BF16)
    embed, logits = pl.pallas_call(
        kernel,
        out_shape=(
            jax.ShapeDtypeStruct((8, D), F32),
            jax.ShapeDtypeStruct((2 * NQ, NX), BF16),
        ),
        in_specs=[hbm] * 10,
        out_specs=(vmem, vmem),
        scratch_shapes=[
            pltpu.VMEM((3, 4, NX, D), BF16),
            pltpu.VMEM((3, 9, D, D), BF16),
            pltpu.VMEM((QRY, 8, D), F32),
            pltpu.VMEM((QRY, 16, 128), BF16),
            square,
            square,
            square,
            square,
            pltpu.VMEM((D, D), BF16),
            pltpu.VMEM((1, D), F32),
            pltpu.VMEM((MB, NQ), jnp.int32),
            square,
            square,
            pltpu.VMEM((2 * NX, D), BF16),
            pltpu.VMEM((D, 2 * NX), BF16),
            square,
            square,
            pltpu.VMEM((LAYERS, SPAN, 8, 128), F32),
            pltpu.VMEM((LAYERS, 2, QRY, 16, 128), BF16),
            pltpu.VMEM((LAYERS, 2, QRY, 16, 128), BF16),
            pltpu.VMEM((LAYERS, QRY, 16, 128), BF16),
            pltpu.VMEM((NQ, D), F32),
            pltpu.VMEM((3, 2 * NX, D), F32),
            pltpu.VMEM((MB * NQ, QRY * 64), BF16),
            pltpu.VMEM((MB * NQ, QRY * 16), BF16),
            pltpu.VMEM((2 * NQ, NX), F32),
            dma((9,)),
            dma((3,)),
            dma((6 * CHUNKS + 2,)),
            dma((6 * CHUNKS + 2,)),
            dma,
            dma,
            dma,
            dma,
            dma((LAYERS,)),
            dma((LAYERS, 4)),
            dma((LAYERS, 4)),
            dma((LAYERS, 4)),
            dma((LAYERS,)),
            dma((LAYERS,)),
            pltpu.SemaphoreType.REGULAR((2,)),
        ],
        compiler_params=pltpu.CompilerParams(
            collective_id=0, has_side_effects=True, vmem_limit_bytes=40 * 1024 * 1024
        ),
    )(
        *(
            pltpu.with_memory_space_constraint(operand, pltpu.HBM)
            for operand in (
                features,
                conv_weight.reshape(9, 3, D, D),
                queries,
                w_query,
                w_key,
                w_value,
                w_out,
                norm_gain.reshape(1, D),
                mask_weight,
                mask_blocks.T,
            )
        )
    )
    embed, logits = pl.pallas_call(
        hand_over,
        out_shape=(
            jax.ShapeDtypeStruct((8, D), F32),
            jax.ShapeDtypeStruct((2 * NQ, NX), BF16),
        ),
        in_specs=[vmem] * 2,
        out_specs=(pl.BlockSpec(memory_space=pl.ANY),) * 2,
        scratch_shapes=[dma((2,))],
    )(*(pltpu.with_memory_space_constraint(part, pltpu.VMEM) for part in (embed, logits)))
    return embed, logits.reshape(NQ, 1, 2, NX)


def solution(mesh):
    return jax.shard_map(
        local,
        mesh=mesh,
        in_specs=(
            P("span", "qry", None, None),
            P(),
            P("qry", None),
            P(),
            P(),
            P(),
            P(),
            P(),
            P(),
            P(),
        ),
        out_specs=(P("qry", None), P(None, "span", "qry", None)),
        check_vma=False,
    )
```
